128 devices in a mesh: cluster: 8 (over y, core), member: 16 (over z, x).
Axes of the slice: x: 4, y: 4, z: 4, core: 2. Of those that a mesh axis runs over, the one named last changes fastest.
Arguments:
- features: bfloat16 [131072, 512], P(('cluster', 'member')), may hold values from -6 to 6
- aggregated: bfloat16 [131072, 512], P(('cluster', 'member')), may hold values from -6 to 6
- cotangent: bfloat16 [131072, 512], P(('cluster', 'member')), may hold values from -6 to 6
- w_self: bfloat16 [512, 512], replicated, may hold values from -0.25 to 0.25
- w_neigh: bfloat16 [512, 512], replicated, may hold values from -0.25 to 0.25
- degrees: int32 [131072], P(('cluster', 'member')), may hold values from 16 to 128
- tile_rows: int32 [49152], P(('cluster', 'member')), may hold values from 0 to 7
- tile_cols: int32 [49152], P(('cluster', 'member')), may hold values from 0 to 15, as said below
- tile_vals: bfloat16 [49152, 128, 128], P(('cluster', 'member')), may hold values from 0 to 1
- recv_rows: int32 [128, 128, 16], P(('cluster', 'member')), may hold values from 0 to 1024, as said below
Outputs:
- grad_nodes: float32 [131072, 512], P(('cluster', 'member'))
- grad_hubs: float32 [2048, 512], P(('cluster', 'member'))
- grad_weights: float32 [2, 512, 512], replicated
The draws below stay inside these ranges and needn't reach their ends.
Inputs may be any that keep to these rules, and one draw needn't show every extreme that they name: `tile_cols`: tiles of the hub region name blocks below 16, own tiles below 8, boundary tiles below 16. `recv_rows`: every receiver gets 16 live rows from some sender; live rows of a sender come first.
All inputs are finite; a program needn't handle non-finite values.
Results may differ from the reference program's by a relative error of at most 0.0029.
Values may be sent and summed in bfloat16 or wider, within the bound.
No kernel may reach another device: no remote copies, remote signals or barrier semaphores. Data moves between devices by JAX's collectives and lax.ppermute only.
A program may use at most 192 MiB of HBM per device.

```python
import jax
import jax.numpy as jnp
from jax import lax

D = 512
TILE = 128
NODE_DEV = 1024
HUBS = 2048
TILE_REG = 128
SLOT = 16
NODES = 131072
TILES_ALL = 49152
N_CLUSTER = 8
N_MEMBER = 16


def draw_tile_cols(key, part):
    key = jax.random.fold_in(key, 11)
    devices_all = N_CLUSTER * N_MEMBER
    limits = jnp.array([HUBS // 128, NODE_DEV // 128, devices_all * SLOT // 128], jnp.int32)
    bound = jnp.broadcast_to(limits[None, :, None], (devices_all, 3, TILE_REG))
    picks = jax.random.randint(key, (devices_all, 3, TILE_REG), 0, 1 << 20)
    return (picks % bound).reshape(-1).astype(jnp.int32)


def draw_recv_rows(key, part):
    key = jax.random.fold_in(key, 23)
    devices_all = N_CLUSTER * N_MEMBER
    key_count, key_rows = jax.random.split(key)
    counts = jax.random.randint(key_count, (devices_all, devices_all), SLOT // 4, SLOT + 1)
    receiver = jnp.arange(devices_all, dtype=jnp.int32)[:, None]
    sender = jnp.arange(devices_all, dtype=jnp.int32)[None, :]
    counts = jnp.where(sender == (receiver + 1) % devices_all, SLOT, counts)
    rows = jax.random.randint(key_rows, (devices_all, devices_all, SLOT), 0, NODE_DEV)
    slot = jnp.arange(SLOT, dtype=jnp.int32)[None, None, :]
    return jnp.where(slot < counts[:, :, None], rows, NODE_DEV).astype(jnp.int32)


def touch_ends(result, stream_key, least, largest):
    extent = result.shape
    place = [jax.random.randint(jax.random.fold_in(stream_key, axis), (), 0, extent[axis]) for axis in range(len(extent))]
    result = result.at[tuple(place)].set(least)
    longest = extent.index(max(extent))
    place[longest] = (place[longest] + 1) % extent[longest]
    return result.at[tuple(place)].set(largest)


def shard_levels(rng, dims, cuts, low, largest):
    def one(dim, shards_of):
        steps = jax.random.uniform(jax.random.fold_in(jax.random.fold_in(rng, 6), dim), (shards_of,), jnp.float32, low / len(cuts), largest / len(cuts))
        return jnp.repeat(jnp.exp(steps), dims[dim] // shards_of).reshape((-1,) + (1,) * (len(dims) - dim - 1))

    level = one(*cuts[0])
    for cut in cuts[1:]:
        level = level * one(*cut)
    return level


def normal_values(rng, dims, scale, most, cuts=(), kind=jnp.bfloat16):
    loudness = shard_levels(rng, dims, cuts, -0.22, 0.18) if cuts else 1.0
    drawn = jax.random.normal(rng, dims, jnp.float32) * scale * loudness
    return jnp.minimum(jnp.maximum(drawn, -most), most).astype(kind)


def setup_inputs(seed: int = 0) -> dict:
    streams_of = jax.random.split(jax.random.key(seed), 11)
    return {
        "features": normal_values(streams_of[0], (NODES, D), 1.0, 6.0, ((0, 128),)),
        "aggregated": normal_values(streams_of[1], (NODES, D), 1.0, 6.0, ((0, 128),)),
        "cotangent": normal_values(streams_of[2], (NODES, D), 1.0, 6.0, ((0, 128),)),
        "w_self": normal_values(streams_of[3], (D, D), D ** -0.5, 0.25),
        "w_neigh": normal_values(streams_of[4], (D, D), D ** -0.5, 0.25),
        "degrees": touch_ends(jax.random.randint(streams_of[5], (NODES,), 16, 129), jax.random.fold_in(streams_of[5], 1), 16, 128).astype(jnp.int32),
        "tile_rows": touch_ends(jax.random.randint(streams_of[6], (TILES_ALL,), 0, NODE_DEV // 128), jax.random.fold_in(streams_of[6], 1), 0, (NODE_DEV // 128) - 1).astype(jnp.int32),
        "tile_cols": draw_tile_cols(jax.random.fold_in(streams_of[10], 71), 0),
        "tile_vals": jnp.clip(1.0 * jax.random.uniform(streams_of[8], (TILES_ALL, TILE, TILE), jnp.float32) ** shard_levels(streams_of[8], (TILES_ALL, TILE, TILE), ((0, 128),), -0.2, 0.2), 0.0, 1.0).astype(jnp.bfloat16),
        "recv_rows": draw_recv_rows(jax.random.fold_in(streams_of[10], 71), 0),
    }


def spread(vals, rows, cols, msg_blocks, nblocks):
    width = msg_blocks.shape[2]
    acc = jnp.zeros((nblocks, 128, width), jnp.float32)
    count = vals.shape[0]
    step = min(32, count)
    for start in range(0, count, step):
        gathered = msg_blocks[rows[start:start + step]].astype(jnp.float32)
        prod = jnp.einsum('tij,tid->tjd', vals[start:start + step].astype(jnp.float32), gathered)
        acc = acc.at[cols[start:start + step]].add(prod)
    return acc.reshape(nblocks * 128, width)


def reference(features, aggregated, cotangent, w_self, w_neigh, degrees, tile_rows, tile_cols, tile_vals, recv_rows):
    devices_all = N_CLUSTER * N_MEMBER
    reg = TILE_REG
    tiles_dev = 3 * reg

    def one_device(hub_total, index):
        cot = lax.dynamic_slice_in_dim(cotangent, index * NODE_DEV, NODE_DEV, 0)
        deg = lax.dynamic_slice_in_dim(degrees, index * NODE_DEV, NODE_DEV, 0)
        rows = lax.dynamic_slice_in_dim(tile_rows, index * tiles_dev, tiles_dev, 0)
        cols = lax.dynamic_slice_in_dim(tile_cols, index * tiles_dev, tiles_dev, 0)
        vals = lax.dynamic_slice_in_dim(tile_vals, index * tiles_dev, tiles_dev, 0)
        message = (jnp.dot(cot, w_neigh.T, preferred_element_type=jnp.float32) / deg[:, None].astype(jnp.float32)).astype(jnp.bfloat16)
        msg_blocks = message.reshape(NODE_DEV // 128, 128, D)
        hub_part = spread(vals[:reg], rows[:reg], cols[:reg], msg_blocks, HUBS // 128)
        own_part = spread(vals[reg:2 * reg], rows[reg:2 * reg], cols[reg:2 * reg], msg_blocks, NODE_DEV // 128)
        own_part = own_part + jnp.dot(cot, w_self.T, preferred_element_type=jnp.float32)
        ghost = spread(vals[2 * reg:], rows[2 * reg:], cols[2 * reg:], msg_blocks, devices_all * SLOT // 128)
        ghost = ghost.astype(jnp.bfloat16).reshape(devices_all, SLOT, D)
        return hub_total + hub_part, (own_part, ghost)

    hub_total, (own_all, ghost_all) = lax.scan(one_device, jnp.zeros((HUBS, D), jnp.float32), jnp.arange(devices_all, dtype=jnp.int32))

    def receive(index):
        arrived = ghost_all[:, index].astype(jnp.float32).reshape(devices_all * SLOT, D)
        targets = recv_rows[index].reshape(-1)
        padded = jnp.zeros((NODE_DEV + 1, D), jnp.float32).at[targets].add(arrived)
        return own_all[index] + padded[:NODE_DEV]

    grad_nodes = lax.map(receive, jnp.arange(devices_all, dtype=jnp.int32)).reshape(devices_all * NODE_DEV, D)
    self_grad = jnp.einsum('nd,ne->de', features.astype(jnp.float32), cotangent.astype(jnp.float32))
    neigh_grad = jnp.einsum('nd,ne->de', aggregated.astype(jnp.float32), cotangent.astype(jnp.float32))
    return grad_nodes, hub_total, jnp.stack([self_grad, neigh_grad])
```

```python
import functools

import jax
import jax.numpy as jnp
from jax import lax
from jax.experimental import pallas as pl
from jax.experimental.pallas import tpu as pltpu
from jax.sharding import Mesh, PartitionSpec as P

F32 = jnp.float32
BF16 = jnp.bfloat16
ALL = ("y", "core", "z", "x")
TILE = 128
REG = 128
WIDTH = 512
NODES = 1024
HUB_BLOCKS = 16
OWN_BLOCKS = 8
UNROLL = 8
PLAN = 256
VMEM = 56 << 20


def contract(a, b, da, db):
    return lax.dot_general(a, b, (((da,), (db,)), ((), ())), preferred_element_type=F32)


def write_plan(region, rows_ref, cols_ref, plan_vmem, blocks):
    cols = cols_ref[region : region + 1, :]
    rows = rows_ref[region : region + 1, :]
    hot = (lax.broadcasted_iota(jnp.int32, (16, REG), 0) == cols).astype(F32)
    before = (
        lax.broadcasted_iota(jnp.int32, (REG, REG), 0) < lax.broadcasted_iota(jnp.int32, (REG, REG), 1)
    ).astype(BF16)
    rank = jnp.sum(hot * contract(hot.astype(BF16), before, 1, 0), axis=0, keepdims=True)
    counts = jnp.sum(hot, axis=1, keepdims=True)
    groups = jnp.floor((counts + 1.0) * 0.5)
    upto = (
        lax.broadcasted_iota(jnp.int32, (16, 16), 1) <= lax.broadcasted_iota(jnp.int32, (16, 16), 0)
    ).astype(BF16)
    ends = contract(upto, jnp.broadcast_to(groups, (16, REG)).astype(BF16), 1, 0)
    starts = ends - groups
    slot = 2.0 * jnp.sum(hot * starts, axis=0, keepdims=True) + rank
    match = (lax.broadcasted_iota(jnp.int32, (PLAN, REG), 0) == slot.astype(jnp.int32)).astype(BF16)
    which = lax.broadcasted_iota(jnp.int32, (8, REG), 1).astype(F32) - REG
    line = lax.broadcasted_iota(jnp.int32, (8, REG), 0)
    values = jnp.where(line == 0, which, jnp.where(line == 1, rows.astype(F32), 0.0))
    slots = contract(values.astype(BF16), match, 1, 1)
    group = lax.broadcasted_iota(jnp.int32, (16, REG), 1).astype(F32)
    column = jnp.sum((ends <= group).astype(F32), axis=0, keepdims=True)
    column = jnp.minimum(column, blocks - 1.0)
    column = jnp.concatenate([column, column], axis=1)
    line = lax.broadcasted_iota(jnp.int32, (8, PLAN), 0)
    plan_vmem[...] = jnp.where(line == 2, column, slots).astype(jnp.int32)


def tile_products(blocks, plan, vals, msg_ref, acc):
    groups = (REG + blocks) // 2

    def one(g):
        first = plan[0, 2 * g] + REG
        second = plan[0, 2 * g + 1] + REG
        row_a = pl.multiple_of(plan[1, 2 * g] * TILE, TILE)
        row_b = pl.multiple_of(plan[1, 2 * g + 1] * TILE, TILE)
        lhs = jnp.concatenate([vals[first], vals[second]], axis=0)
        rhs = jnp.concatenate([msg_ref[pl.ds(row_a, TILE), :], msg_ref[pl.ds(row_b, TILE), :]], axis=0)
        place = pl.ds(pl.multiple_of(plan[2, g] * TILE, TILE), TILE)
        acc[place, :] += contract(lhs, rhs, 0, 0)

    def body(step, carry):
        for k in range(UNROLL):
            one(step * UNROLL + k)
        return carry

    lax.fori_loop(0, groups // UNROLL, body, 0)
    for g in range(groups // UNROLL * UNROLL, groups):
        one(g)


def load_tiles(region, vals_hbm, vals, sem):
    copy = pltpu.make_async_copy(vals_hbm.at[pl.ds(region * REG, REG)], vals.at[pl.ds(0, REG)], sem)
    copy.start()
    vals[REG] = jnp.zeros((TILE, TILE), BF16)
    return copy


def make_plan(region, rows_ref, cols_ref, plan_vmem, plan, plan_sem, blocks):
    write_plan(region, rows_ref, cols_ref, plan_vmem, blocks)
    copy = pltpu.make_async_copy(plan_vmem, plan, plan_sem)
    copy.start()
    return copy


def hub_kernel(core, rows_ref, cols_ref, deg_ref, cot_ref, w_ref, vals_hbm, msg_ref, keep_ref, send_ref,
               vals, acc, plan_vmem, plan, sem, plan_sem):
    tiles = load_tiles(0, vals_hbm, vals, sem)
    ready = make_plan(0, rows_ref, cols_ref, plan_vmem, plan, plan_sem, HUB_BLOCKS)
    scale = jnp.transpose(1.0 / deg_ref[...].astype(F32))
    for r in range(NODES // TILE):
        part = contract(cot_ref[r * TILE : (r + 1) * TILE, :], w_ref[...], 1, 1)
        msg_ref[r * TILE : (r + 1) * TILE, :] = (part * scale[:, r : r + 1]).astype(BF16)
    acc[...] = jnp.zeros_like(acc)
    ready.wait()
    tiles.wait()
    tile_products(HUB_BLOCKS, plan, vals, msg_ref, acc)
    half = WIDTH // 2

    @pl.when(core[0] == 0)
    def _():
        keep_ref[...] = acc[:, :half]
        send_ref[...] = acc[:, half:]

    @pl.when(core[0] != 0)
    def _():
        keep_ref[...] = acc[:, half:]
        send_ref[...] = acc[:, :half]


def ghost_kernel(rows_ref, cols_ref, msg_ref, vals_hbm, out_ref, vals, acc, plan_vmem, plan, sem, plan_sem):
    tiles = load_tiles(2, vals_hbm, vals, sem)
    ready = make_plan(2, rows_ref, cols_ref, plan_vmem, plan, plan_sem, HUB_BLOCKS)
    acc[...] = jnp.zeros_like(acc)
    ready.wait()
    tiles.wait()
    tile_products(HUB_BLOCKS, plan, vals, msg_ref, acc)
    out_ref[...] = acc[...].astype(BF16)


def own_kernel(rows_ref, cols_ref, msg_ref, cot_ref, w_ref, vals_hbm, out_ref, vals, plan_vmem, plan, sem, plan_sem):
    tiles = load_tiles(1, vals_hbm, vals, sem)
    ready = make_plan(1, rows_ref, cols_ref, plan_vmem, plan, plan_sem, OWN_BLOCKS)
    for r in range(NODES // TILE):
        block = slice(r * TILE, (r + 1) * TILE)
        out_ref[block, :] = contract(cot_ref[block, :], w_ref[...], 1, 1)
    ready.wait()
    tiles.wait()
    tile_products(OWN_BLOCKS, plan, vals, msg_ref, out_ref)


def pack_kernel(keep_ref, came_ref, packed_hbm, out_ref):
    del packed_hbm
    out_ref[...] = (keep_ref[...] + came_ref[...]).astype(BF16)


def weights_kernel(core, feat_ref, agg_ref, cot_ref, keep_ref, send_ref):
    @pl.when(core[0] == 0)
    def _():
        keep_ref[...] = contract(feat_ref[...], cot_ref[...], 0, 0)
        send_ref[...] = contract(agg_ref[...], cot_ref[...], 0, 0)

    @pl.when(core[0] != 0)
    def _():
        keep_ref[...] = contract(agg_ref[...], cot_ref[...], 0, 0)
        send_ref[...] = contract(feat_ref[...], cot_ref[...], 0, 0)


def landing_kernel(targets_ref, own_ref, arrived_ref, nodes_ref, hubs_ref):
    chunk = 256
    slots = arrived_ref.shape[0]
    for s in range(slots // chunk):
        goal = targets_ref[s : s + 1, :]
        place = (lax.broadcasted_iota(jnp.int32, (NODES, chunk), 0) == goal).astype(BF16)
        part = contract(place, arrived_ref[s * chunk : (s + 1) * chunk, :WIDTH], 1, 0)
        if s == 0:
            nodes_ref[...] = own_ref[...] + part
        else:
            nodes_ref[...] += part
    half = WIDTH // 2
    for c in range(2):
        total = jnp.zeros((16, half), F32)
        for y in range(4):
            start = (2 * y + c) * 256
            for m in range(16):
                total += arrived_ref[start + 16 * m : start + 16 * m + 16, WIDTH:].astype(F32)
        hubs_ref[:, c * half : (c + 1) * half] = total


def whole(*shape):
    return pl.BlockSpec(shape, lambda i, *_: (0,) * len(shape))


ANY = pl.BlockSpec(memory_space=pl.ANY)


def call(kernel, name, scalars, ins, outs, shapes, scratch, flops, moved, **more):
    return pl.pallas_call(
        kernel,
        grid_spec=pltpu.PrefetchScalarGridSpec(
            num_scalar_prefetch=scalars, grid=(1,), in_specs=ins, out_specs=outs, scratch_shapes=scratch
        ),
        out_shape=shapes,
        compiler_params=pltpu.CompilerParams(vmem_limit_bytes=VMEM),
        cost_estimate=pl.CostEstimate(flops=flops, bytes_accessed=moved, transcendentals=0),
        name=name,
        **more,
    )


def tile_scratch(acc):
    kept = [pltpu.VMEM((REG + 1, TILE, TILE), BF16)]
    if acc:
        kept.append(pltpu.VMEM((HUB_BLOCKS * TILE, WIDTH), F32))
    return kept + [
        pltpu.VMEM((8, PLAN), jnp.int32),
        pltpu.SMEM((8, PLAN), jnp.int32),
        pltpu.SemaphoreType.DMA,
        pltpu.SemaphoreType.DMA,
    ]


def shift(k, n):
    return [(i, (i + k) % n) for i in range(n)]


def others(pieces, axis):
    return [lax.ppermute(pieces(k), axis, shift(k, 4)) for k in (1, 2, 3)]


def scatter_sum(x, axis, kind):
    me = lax.axis_index(axis)
    parts = x.reshape(4, x.shape[0] // 4, x.shape[1])

    def piece(k):
        return lax.dynamic_index_in_dim(parts, (me + k) % 4, 0, keepdims=False).astype(kind)

    came = others(piece, axis)
    total = lax.dynamic_index_in_dim(parts, me, 0, keepdims=False)
    for part in came:
        total = total + part.astype(F32)
    return total


def by_index(mine, came, axis):
    me = lax.axis_index(axis)
    held = [mine] + came
    out = []
    for i in range(4):
        back = (me - i) % 4
        pick = held[0]
        for k in (1, 2, 3):
            pick = jnp.where(back == k, held[k], pick)
        out.append(pick)
    return out


def gather(x, axis):
    return jnp.concatenate(by_index(x, others(lambda k: x, axis), axis), axis=0)


def all_sum(x, axis):
    a, b, c, d = by_index(x, others(lambda k: x, axis), axis)
    return (a + b) + (c + d)


def local(features, aggregated, cotangent, w_self, w_neigh, degrees, tile_rows, tile_cols, tile_vals, recv_rows):
    core = lax.axis_index("core")
    core_arg = core.reshape(1).astype(jnp.int32)
    rows = tile_rows.reshape(3, REG)
    cols = tile_cols.reshape(3, REG)
    deg = degrees.reshape(NODES // TILE, TILE)
    targets = recv_rows.reshape(8, 256)
    half = WIDTH // 2
    spec_rc = whole(3, REG)
    spec_nodes = whole(NODES, WIDTH)
    spec_w = whole(WIDTH, WIDTH)
    slots = HUB_BLOCKS * TILE
    region_flops = 2 * REG * TILE * TILE * WIDTH
    region_bytes = REG * TILE * TILE * 2 + NODES * WIDTH * 2 + slots * WIDTH * 2

    w_keep, w_send = call(
        weights_kernel, "weights", 1, [spec_nodes] * 3, [spec_w] * 2,
        [jax.ShapeDtypeStruct((WIDTH, WIDTH), F32)] * 2, [], 4 * NODES * WIDTH * WIDTH, 5 << 20,
    )(core_arg, features, aggregated, cotangent)
    w_came = lax.ppermute(w_send, "core", shift(1, 2))

    msg, hub_keep, hub_send = call(
        hub_kernel, "hub", 1,
        [spec_rc, spec_rc, whole(8, TILE), spec_nodes, spec_w, ANY],
        [spec_nodes, whole(slots, half), whole(slots, half)],
        [
            jax.ShapeDtypeStruct((NODES, WIDTH), BF16),
            jax.ShapeDtypeStruct((slots, half), F32),
            jax.ShapeDtypeStruct((slots, half), F32),
        ],
        tile_scratch(True), region_flops + 2 * NODES * WIDTH * WIDTH, region_bytes + (2 << 20),
    )(core_arg, rows, cols, deg, cotangent, w_neigh, tile_vals)
    hub_came = lax.ppermute(hub_send, "core", shift(1, 2))

    packed = call(
        ghost_kernel, "ghost", 0, [spec_rc, spec_rc, spec_nodes, ANY], whole(slots, WIDTH),
        jax.ShapeDtypeStruct((slots, WIDTH + half), BF16),
        tile_scratch(True), region_flops, region_bytes,
    )(rows, cols, msg, tile_vals)
    packed = call(
        pack_kernel, "pack", 0, [whole(slots, half), whole(slots, half), ANY],
        pl.BlockSpec((slots, half), lambda i: (0, 2)),
        jax.ShapeDtypeStruct((slots, WIDTH + half), BF16),
        [], slots * half, 5 << 20, input_output_aliases={2: 0},
    )(hub_keep, hub_came, packed)
    arrived = lax.all_to_all(
        packed.reshape(128, 16, WIDTH + half), ALL, split_axis=0, concat_axis=0, tiled=True
    ).reshape(slots, WIDTH + half)

    own = call(
        own_kernel, "own", 0, [spec_rc, spec_rc, spec_nodes, spec_nodes, spec_w, ANY], spec_nodes,
        jax.ShapeDtypeStruct((NODES, WIDTH), F32),
        tile_scratch(False), region_flops + 2 * NODES * WIDTH * WIDTH, region_bytes,
    )(rows, cols, msg, cotangent, w_self, tile_vals)

    mine = w_keep + w_came
    mine = scatter_sum(mine, "x", BF16)
    mine = scatter_sum(mine, "z", F32)
    mine = all_sum(mine, "y").astype(BF16)
    mine = gather(gather(mine, "z"), "x")
    other = lax.ppermute(mine, "core", shift(1, 2))
    grad_weights = jnp.where(
        core == 0, jnp.stack([mine, other]), jnp.stack([other, mine])
    ).astype(F32)

    grad_nodes, grad_hubs = call(
        landing_kernel, "landing", 0,
        [whole(8, 256), spec_nodes, whole(slots, WIDTH + half)],
        [spec_nodes, whole(16, WIDTH)],
        [jax.ShapeDtypeStruct((NODES, WIDTH), F32), jax.ShapeDtypeStruct((16, WIDTH), F32)],
        [], 2 * slots * NODES * WIDTH, 7 << 20,
    )(targets, own, arrived)
    return (grad_nodes, grad_hubs, grad_weights)


def solution(mesh):
    fine = Mesh(mesh.devices.reshape(4, 2, 4, 4), ALL)
    rows = P(ALL, None)
    in_specs = (
        rows, rows, rows, P(), P(), P(ALL), P(ALL), P(ALL), P(ALL, None, None), P(ALL, None, None),
    )
    out_specs = (rows, rows, P())
    return jax.shard_map(local, mesh=fine, in_specs=in_specs, out_specs=out_specs, check_vma=False)
```

```python
import functools

import jax
import jax.numpy as jnp
from jax import lax
from jax.experimental import pallas as pl
from jax.experimental.pallas import tpu as pltpu
from jax.sharding import Mesh, PartitionSpec as P

F32 = jnp.float32
BF16 = jnp.bfloat16
ALL = ("y", "core", "z", "x")
TILE = 128
REG = 128
WIDTH = 512
NODES = 1024
HUB_BLOCKS = 16
OWN_BLOCKS = 8
UNROLL = 8
PLAN = 256
VMEM = 56 << 20


def contract(a, b, da, db):
    return lax.dot_general(a, b, (((da,), (db,)), ((), ())), preferred_element_type=F32)


def write_plan(region, rows_ref, cols_ref, plan_vmem, blocks):
    cols = cols_ref[region : region + 1, :]
    rows = rows_ref[region : region + 1, :]
    hot = (lax.broadcasted_iota(jnp.int32, (16, REG), 0) == cols).astype(F32)
    before = (
        lax.broadcasted_iota(jnp.int32, (REG, REG), 0) < lax.broadcasted_iota(jnp.int32, (REG, REG), 1)
    ).astype(BF16)
    rank = jnp.sum(hot * contract(hot.astype(BF16), before, 1, 0), axis=0, keepdims=True)
    counts = jnp.sum(hot, axis=1, keepdims=True)
    groups = jnp.floor((counts + 1.0) * 0.5)
    upto = (
        lax.broadcasted_iota(jnp.int32, (16, 16), 1) <= lax.broadcasted_iota(jnp.int32, (16, 16), 0)
    ).astype(BF16)
    ends = contract(upto, jnp.broadcast_to(groups, (16, REG)).astype(BF16), 1, 0)
    starts = ends - groups
    slot = 2.0 * jnp.sum(hot * starts, axis=0, keepdims=True) + rank
    match = (lax.broadcasted_iota(jnp.int32, (PLAN, REG), 0) == slot.astype(jnp.int32)).astype(BF16)
    which = lax.broadcasted_iota(jnp.int32, (8, REG), 1).astype(F32) - REG
    line = lax.broadcasted_iota(jnp.int32, (8, REG), 0)
    values = jnp.where(line == 0, which, jnp.where(line == 1, rows.astype(F32), 0.0))
    slots = contract(values.astype(BF16), match, 1, 1)
    group = lax.broadcasted_iota(jnp.int32, (16, REG), 1).astype(F32)
    column = jnp.sum((ends <= group).astype(F32), axis=0, keepdims=True)
    column = jnp.minimum(column, blocks - 1.0)
    column = jnp.concatenate([column, column], axis=1)
    line = lax.broadcasted_iota(jnp.int32, (8, PLAN), 0)
    plan_vmem[...] = jnp.where(line == 2, column, slots).astype(jnp.int32)


def tile_products(blocks, plan, vals, msg_ref, acc):
    groups = (REG + blocks) // 2

    def one(g):
        first = plan[0, 2 * g] + REG
        second = plan[0, 2 * g + 1] + REG
        row_a = pl.multiple_of(plan[1, 2 * g] * TILE, TILE)
        row_b = pl.multiple_of(plan[1, 2 * g + 1] * TILE, TILE)
        lhs = jnp.concatenate([vals[first], vals[second]], axis=0)
        rhs = jnp.concatenate([msg_ref[pl.ds(row_a, TILE), :], msg_ref[pl.ds(row_b, TILE), :]], axis=0)
        place = pl.ds(pl.multiple_of(plan[2, g] * TILE, TILE), TILE)
        acc[place, :] += contract(lhs, rhs, 0, 0)

    def body(step, carry):
        for k in range(UNROLL):
            one(step * UNROLL + k)
        return carry

    lax.fori_loop(0, groups // UNROLL, body, 0)
    for g in range(groups // UNROLL * UNROLL, groups):
        one(g)


def load_tiles(region, vals_hbm, vals, sem):
    copy = pltpu.make_async_copy(vals_hbm.at[pl.ds(region * REG, REG)], vals.at[pl.ds(0, REG)], sem)
    copy.start()
    vals[REG] = jnp.zeros((TILE, TILE), BF16)
    return copy


def make_plan(region, rows_ref, cols_ref, plan_vmem, plan, plan_sem, blocks):
    write_plan(region, rows_ref, cols_ref, plan_vmem, blocks)
    copy = pltpu.make_async_copy(plan_vmem, plan, plan_sem)
    copy.start()
    return copy


def ghost_kernel(rows_ref, cols_ref, deg_ref, cot_ref, w_ref, vals_hbm, msg_ref, out_ref,
                 vals, acc, plan_vmem, plan, sem, plan_sem):
    tiles = load_tiles(2, vals_hbm, vals, sem)
    ready = make_plan(2, rows_ref, cols_ref, plan_vmem, plan, plan_sem, HUB_BLOCKS)
    scale = jnp.transpose(1.0 / deg_ref[...].astype(F32))
    for r in range(NODES // TILE):
        part = contract(cot_ref[r * TILE : (r + 1) * TILE, :], w_ref[...], 1, 1)
        msg_ref[r * TILE : (r + 1) * TILE, :] = (part * scale[:, r : r + 1]).astype(BF16)
    acc[...] = jnp.zeros_like(acc)
    ready.wait()
    tiles.wait()
    tile_products(HUB_BLOCKS, plan, vals, msg_ref, acc)
    out_ref[...] = acc[...].astype(BF16)


def hub_kernel(core, rows_ref, cols_ref, msg_ref, vals_hbm, keep_ref, send_ref,
               vals, acc, plan_vmem, plan, sem, plan_sem):
    tiles = load_tiles(0, vals_hbm, vals, sem)
    ready = make_plan(0, rows_ref, cols_ref, plan_vmem, plan, plan_sem, HUB_BLOCKS)
    acc[...] = jnp.zeros_like(acc)
    ready.wait()
    tiles.wait()
    tile_products(HUB_BLOCKS, plan, vals, msg_ref, acc)
    for y in range(4):
        mine = pl.multiple_of((2 * y + core[0]) * 256, 256)
        theirs = pl.multiple_of((2 * y + 1 - core[0]) * 256, 256)
        keep_ref[y * 256 : (y + 1) * 256, :] = acc[pl.ds(mine, 256), :]
        send_ref[y * 256 : (y + 1) * 256, :] = acc[pl.ds(theirs, 256), :]


def own_kernel(rows_ref, cols_ref, msg_ref, cot_ref, w_ref, vals_hbm, out_ref, vals, plan_vmem, plan, sem, plan_sem):
    tiles = load_tiles(1, vals_hbm, vals, sem)
    ready = make_plan(1, rows_ref, cols_ref, plan_vmem, plan, plan_sem, OWN_BLOCKS)
    for r in range(NODES // TILE):
        block = slice(r * TILE, (r + 1) * TILE)
        out_ref[block, :] = contract(cot_ref[block, :], w_ref[...], 1, 1)
    ready.wait()
    tiles.wait()
    tile_products(OWN_BLOCKS, plan, vals, msg_ref, out_ref)


def pack_kernel(keep_ref, came_ref, packed_hbm, out_ref):
    del packed_hbm
    out_ref[...] = (keep_ref[...] + came_ref[...]).astype(BF16)


def hub_pack_kernel(keep_ref, came_ref, out_ref):
    out_ref[...] = (keep_ref[...] + came_ref[...]).astype(BF16)


def weights_kernel(core, feat_ref, agg_ref, cot_ref, keep_ref, send_ref, acc):
    step = pl.program_id(0)
    first = contract(feat_ref[...], cot_ref[...], 0, 0)
    second = contract(agg_ref[...], cot_ref[...], 0, 0)

    @pl.when(step == 0)
    def _():
        acc[:WIDTH] = first
        acc[WIDTH:] = second

    @pl.when(step != 0)
    def _():
        acc[:WIDTH] += first
        acc[WIDTH:] += second

    def put(ref, column):
        for k in range(2):
            ref[k * 2 * WIDTH : (k + 1) * 2 * WIDTH, :] = acc[:, column + k * TILE : column + (k + 1) * TILE]

    last = step == pl.num_programs(0) - 1

    @pl.when(last & (core[0] == 0))
    def _():
        put(keep_ref, 0)
        put(send_ref, 2 * TILE)

    @pl.when(last & (core[0] != 0))
    def _():
        put(keep_ref, 2 * TILE)
        put(send_ref, 0)


def spread_kernel(arrived_ref, packed_hbm, out_ref):
    del packed_hbm
    for c in range(2):
        total = jnp.zeros((16, TILE), F32)
        for y in range(4):
            for m in range(16):
                start = (2 * y + c) * 256 + 16 * m
                total += arrived_ref[start : start + 16, :].astype(F32)
        total = total.astype(BF16)
        for peer in range(64):
            out_ref[16 * peer : 16 * peer + 16, c * TILE : (c + 1) * TILE] = total


def landing_kernel(targets_ref, own_ref, arrived_ref, nodes_ref):
    chunk = 256
    slots = arrived_ref.shape[0]
    for s in range(slots // chunk):
        goal = targets_ref[s : s + 1, :]
        place = (lax.broadcasted_iota(jnp.int32, (NODES, chunk), 0) == goal).astype(BF16)
        part = contract(place, arrived_ref[s * chunk : (s + 1) * chunk, :], 1, 0)
        if s == 0:
            nodes_ref[...] = own_ref[...] + part
        else:
            nodes_ref[...] += part


def hub_sum_kernel(arrived_ref, hubs_ref):
    total = jnp.zeros((16, WIDTH), F32)
    for p in range(64):
        total += arrived_ref[16 * p : 16 * p + 16, :].astype(F32)
    hubs_ref[...] = total


def join_kernel(core, mine_ref, came_ref, out_ref):
    for ref, part in ((mine_ref, core[0]), (came_ref, 1 - core[0])):
        place = pl.ds(pl.multiple_of(part * 256, 256), 256)
        for y in range(4):
            for c in range(2):
                column = (2 * c + y // 2) * TILE
                block = ref[y * 256 : (y + 1) * 256, c * TILE : (c + 1) * TILE]
                out_ref[y % 2, place, column : column + TILE] = block.astype(F32)


def whole(*shape):
    return pl.BlockSpec(shape, lambda i, *_: (0,) * len(shape))


ANY = pl.BlockSpec(memory_space=pl.ANY)


def call(kernel, name, scalars, ins, outs, shapes, scratch, flops, moved, grid=(1,), **more):
    return pl.pallas_call(
        kernel,
        grid_spec=pltpu.PrefetchScalarGridSpec(
            num_scalar_prefetch=scalars, grid=grid, in_specs=ins, out_specs=outs, scratch_shapes=scratch
        ),
        out_shape=shapes,
        compiler_params=pltpu.CompilerParams(vmem_limit_bytes=VMEM),
        cost_estimate=pl.CostEstimate(flops=flops, bytes_accessed=moved, transcendentals=0),
        name=name,
        **more,
    )


def tile_scratch(acc):
    kept = [pltpu.VMEM((REG + 1, TILE, TILE), BF16)]
    if acc:
        kept.append(pltpu.VMEM((HUB_BLOCKS * TILE, WIDTH), F32))
    return kept + [
        pltpu.VMEM((8, PLAN), jnp.int32),
        pltpu.SMEM((8, PLAN), jnp.int32),
        pltpu.SemaphoreType.DMA,
        pltpu.SemaphoreType.DMA,
    ]


def shift(k, n):
    return [(i, (i + k) % n) for i in range(n)]


def local(features, aggregated, cotangent, w_self, w_neigh, degrees, tile_rows, tile_cols, tile_vals, recv_rows):
    core_arg = lax.axis_index("core").reshape(1).astype(jnp.int32)
    rows = tile_rows.reshape(3, REG)
    cols = tile_cols.reshape(3, REG)
    deg = degrees.reshape(NODES // TILE, TILE)
    targets = recv_rows.reshape(8, 256)
    spec_rc = whole(3, REG)
    spec_nodes = whole(NODES, WIDTH)
    spec_w = whole(WIDTH, WIDTH)
    slots = HUB_BLOCKS * TILE
    region_flops = 2 * REG * TILE * TILE * WIDTH
    region_bytes = REG * TILE * TILE * 2 + NODES * WIDTH * 2 + slots * WIDTH * 2
    swap = shift(1, 2)

    steps = 4
    spec_rows = pl.BlockSpec((NODES // steps, WIDTH), lambda i, *_: (i, 0))
    w_keep, w_send = call(
        weights_kernel, "weights", 1, [spec_rows] * 3, [whole(slots, TILE)] * 2,
        [jax.ShapeDtypeStruct((slots, TILE), F32)] * 2, [pltpu.VMEM((2 * WIDTH, WIDTH), F32)],
        4 * NODES * WIDTH * WIDTH, 5 << 20, grid=(steps,),
    )(core_arg, features, aggregated, cotangent)
    w_came = lax.ppermute(w_send, "core", swap)

    wide = WIDTH + TILE
    msg, packed = call(
        ghost_kernel, "ghost", 0,
        [spec_rc, spec_rc, whole(8, TILE), spec_nodes, spec_w, ANY],
        [spec_nodes, whole(slots, WIDTH)],
        [jax.ShapeDtypeStruct((NODES, WIDTH), BF16), jax.ShapeDtypeStruct((slots, wide), BF16)],
        tile_scratch(True), region_flops + 2 * NODES * WIDTH * WIDTH, region_bytes + (2 << 20),
    )(rows, cols, deg, cotangent, w_neigh, tile_vals)
    spec_part = pl.BlockSpec((slots // steps, TILE), lambda i: (i, 0))
    packed = call(
        pack_kernel, "pack", 0, [spec_part, spec_part, ANY],
        pl.BlockSpec((slots // steps, TILE), lambda i: (i, WIDTH // TILE)),
        jax.ShapeDtypeStruct((slots, wide), BF16),
        [], slots * TILE, 3 << 20, grid=(steps,), input_output_aliases={2: 0},
    )(w_keep, w_came, packed)
    arrived = lax.all_to_all(
        packed.reshape(128, 16, wide), ALL, split_axis=0, concat_axis=0, tiled=True
    ).reshape(slots, wide)

    hub_keep, hub_send = call(
        hub_kernel, "hub", 1, [spec_rc, spec_rc, spec_nodes, ANY], [spec_nodes, spec_nodes],
        [jax.ShapeDtypeStruct((NODES, WIDTH), F32)] * 2,
        tile_scratch(True), region_flops, region_bytes + (2 << 20),
    )(core_arg, rows, cols, msg, tile_vals)
    hub_came = lax.ppermute(hub_send, "core", swap)
    own = call(
        own_kernel, "own", 0, [spec_rc, spec_rc, spec_nodes, spec_nodes, spec_w, ANY], spec_nodes,
        jax.ShapeDtypeStruct((NODES, WIDTH), F32),
        tile_scratch(False), region_flops + 2 * NODES * WIDTH * WIDTH, region_bytes,
    )(rows, cols, msg, cotangent, w_self, tile_vals)

    wider = WIDTH + 2 * TILE
    spec_hub = pl.BlockSpec((NODES // steps, WIDTH), lambda i: (i, 0))
    packed = call(
        hub_pack_kernel, "hub_pack", 0, [spec_hub, spec_hub], spec_hub,
        jax.ShapeDtypeStruct((NODES, wider), BF16), [], NODES * WIDTH, 5 << 20, grid=(steps,),
    )(hub_keep, hub_came)
    packed = call(
        spread_kernel, "spread", 0, [pl.BlockSpec((slots, TILE), lambda i: (0, WIDTH // TILE)), ANY],
        pl.BlockSpec((NODES, 2 * TILE), lambda i: (0, WIDTH // (2 * TILE))),
        jax.ShapeDtypeStruct((NODES, wider), BF16), [], slots * TILE, 1 << 20, input_output_aliases={1: 0},
    )(arrived, packed)
    shared = lax.all_to_all(
        packed.reshape(64, 16, wider), ("y", "z", "x"), split_axis=0, concat_axis=0, tiled=True
    ).reshape(NODES, wider)

    grad_nodes = call(
        landing_kernel, "landing", 0, [whole(8, 256), spec_nodes, whole(slots, WIDTH)], spec_nodes,
        jax.ShapeDtypeStruct((NODES, WIDTH), F32), [], 2 * slots * NODES * WIDTH, 7 << 20,
    )(targets, own, arrived)

    w_mine = shared[:, WIDTH:]
    w_theirs = lax.ppermute(w_mine, "core", swap)
    grad_hubs = call(
        hub_sum_kernel, "hub_sum", 0, [spec_nodes], whole(16, WIDTH),
        jax.ShapeDtypeStruct((16, WIDTH), F32), [], NODES * WIDTH, 1 << 20,
    )(shared)
    grad_weights = call(
        join_kernel, "join", 1, [whole(NODES, 2 * TILE)] * 2, whole(2, WIDTH, WIDTH),
        jax.ShapeDtypeStruct((2, WIDTH, WIDTH), F32), [], NODES * WIDTH, 3 << 20,
    )(core_arg, w_mine, w_theirs)
    return (grad_nodes, grad_hubs, grad_weights)


def solution(mesh):
    fine = Mesh(mesh.devices.reshape(4, 2, 4, 4), ALL)
    rows = P(ALL, None)
    in_specs = (
        rows, rows, rows, P(), P(), P(ALL), P(ALL), P(ALL), P(ALL, None, None), P(ALL, None, None),
    )
    out_specs = (rows, rows, P())
    return jax.shard_map(local, mesh=fine, in_specs=in_specs, out_specs=out_specs, check_vma=False)
```

```python
import functools

import jax
import jax.numpy as jnp
from jax import lax
from jax.experimental import pallas as pl
from jax.experimental.pallas import tpu as pltpu
from jax.sharding import Mesh, PartitionSpec as P

F32 = jnp.float32
BF16 = jnp.bfloat16
ALL = ("y", "core", "z", "x")
TILE = 128
REG = 128
WIDTH = 512
NODES = 1024
HUB_BLOCKS = 16
OWN_BLOCKS = 8
UNROLL = 8
PLAN = 256
VMEM = 56 << 20


def contract(a, b, da, db):
    return lax.dot_general(a, b, (((da,), (db,)), ((), ())), preferred_element_type=F32)


def write_plan(region, rows_ref, cols_ref, plan_vmem, blocks):
    cols = cols_ref[region : region + 1, :]
    rows = rows_ref[region : region + 1, :]
    hot = (lax.broadcasted_iota(jnp.int32, (16, REG), 0) == cols).astype(F32)
    before = (
        lax.broadcasted_iota(jnp.int32, (REG, REG), 0) < lax.broadcasted_iota(jnp.int32, (REG, REG), 1)
    ).astype(BF16)
    rank = jnp.sum(hot * contract(hot.astype(BF16), before, 1, 0), axis=0, keepdims=True)
    counts = jnp.sum(hot, axis=1, keepdims=True)
    groups = jnp.floor((counts + 1.0) * 0.5)
    upto = (
        lax.broadcasted_iota(jnp.int32, (16, 16), 1) <= lax.broadcasted_iota(jnp.int32, (16, 16), 0)
    ).astype(BF16)
    ends = contract(upto, jnp.broadcast_to(groups, (16, REG)).astype(BF16), 1, 0)
    starts = ends - groups
    slot = 2.0 * jnp.sum(hot * starts, axis=0, keepdims=True) + rank
    match = (lax.broadcasted_iota(jnp.int32, (PLAN, REG), 0) == slot.astype(jnp.int32)).astype(BF16)
    which = lax.broadcasted_iota(jnp.int32, (8, REG), 1).astype(F32) - REG
    line = lax.broadcasted_iota(jnp.int32, (8, REG), 0)
    values = jnp.where(line == 0, which, jnp.where(line == 1, rows.astype(F32), 0.0))
    slots = contract(values.astype(BF16), match, 1, 1)
    group = lax.broadcasted_iota(jnp.int32, (16, REG), 1).astype(F32)
    column = jnp.sum((ends <= group).astype(F32), axis=0, keepdims=True)
    column = jnp.minimum(column, blocks - 1.0)
    column = jnp.concatenate([column, column], axis=1)
    line = lax.broadcasted_iota(jnp.int32, (8, PLAN), 0)
    plan_vmem[...] = jnp.where(line == 2, column, slots).astype(jnp.int32)


def tile_products(blocks, plan, vals, msg_ref, acc):
    groups = (REG + blocks) // 2

    def one(g):
        first = plan[0, 2 * g] + REG
        second = plan[0, 2 * g + 1] + REG
        row_a = pl.multiple_of(plan[1, 2 * g] * TILE, TILE)
        row_b = pl.multiple_of(plan[1, 2 * g + 1] * TILE, TILE)
        lhs = jnp.concatenate([vals[first], vals[second]], axis=0)
        rhs = jnp.concatenate([msg_ref[pl.ds(row_a, TILE), :], msg_ref[pl.ds(row_b, TILE), :]], axis=0)
        place = pl.ds(pl.multiple_of(plan[2, g] * TILE, TILE), TILE)
        acc[place, :] += contract(lhs, rhs, 0, 0)

    def body(step, carry):
        for k in range(UNROLL):
            one(step * UNROLL + k)
        return carry

    lax.fori_loop(0, groups // UNROLL, body, 0)
    for g in range(groups // UNROLL * UNROLL, groups):
        one(g)


def load_tiles(region, vals_hbm, vals, sem):
    copy = pltpu.make_async_copy(vals_hbm.at[pl.ds(region * REG, REG)], vals.at[pl.ds(0, REG)], sem)
    copy.start()
    vals[REG] = jnp.zeros((TILE, TILE), BF16)
    return copy


def make_plan(region, rows_ref, cols_ref, plan_vmem, plan, plan_sem, blocks):
    write_plan(region, rows_ref, cols_ref, plan_vmem, blocks)
    copy = pltpu.make_async_copy(plan_vmem, plan, plan_sem)
    copy.start()
    return copy


def ghost_kernel(rows_ref, cols_ref, deg_ref, cot_ref, w_ref, vals_hbm, msg_ref, out_ref,
                 vals, acc, plan_vmem, plan, sem, plan_sem):
    tiles = load_tiles(2, vals_hbm, vals, sem)
    ready = make_plan(2, rows_ref, cols_ref, plan_vmem, plan, plan_sem, HUB_BLOCKS)
    scale = jnp.transpose(1.0 / deg_ref[...].astype(F32))
    for r in range(NODES // TILE):
        part = contract(cot_ref[r * TILE : (r + 1) * TILE, :], w_ref[...], 1, 1)
        msg_ref[r * TILE : (r + 1) * TILE, :] = (part * scale[:, r : r + 1]).astype(BF16)
    acc[...] = jnp.zeros_like(acc)
    ready.wait()
    tiles.wait()
    tile_products(HUB_BLOCKS, plan, vals, msg_ref, acc)
    out_ref[...] = acc[...].astype(BF16)


def hub_kernel(core, rows_ref, cols_ref, msg_ref, vals_hbm, keep_ref, send_ref,
               vals, acc, plan_vmem, plan, sem, plan_sem):
    tiles = load_tiles(0, vals_hbm, vals, sem)
    ready = make_plan(0, rows_ref, cols_ref, plan_vmem, plan, plan_sem, HUB_BLOCKS)
    acc[...] = jnp.zeros_like(acc)
    ready.wait()
    tiles.wait()
    tile_products(HUB_BLOCKS, plan, vals, msg_ref, acc)
    for y in range(4):
        mine = pl.multiple_of((2 * y + core[0]) * 256, 256)
        theirs = pl.multiple_of((2 * y + 1 - core[0]) * 256, 256)
        keep_ref[y * 256 : (y + 1) * 256, :] = acc[pl.ds(mine, 256), :]
        send_ref[y * 256 : (y + 1) * 256, :] = acc[pl.ds(theirs, 256), :]


def own_kernel(rows_ref, cols_ref, msg_ref, cot_ref, w_ref, vals_hbm, out_ref, vals, plan_vmem, plan, sem, plan_sem):
    tiles = load_tiles(1, vals_hbm, vals, sem)
    ready = make_plan(1, rows_ref, cols_ref, plan_vmem, plan, plan_sem, OWN_BLOCKS)
    for r in range(NODES // TILE):
        block = slice(r * TILE, (r + 1) * TILE)
        out_ref[block, :] = contract(cot_ref[block, :], w_ref[...], 1, 1)
    ready.wait()
    tiles.wait()
    tile_products(OWN_BLOCKS, plan, vals, msg_ref, out_ref)


def pack_kernel(keep_ref, came_ref, packed_hbm, out_ref):
    del packed_hbm
    out_ref[...] = (keep_ref[...] + came_ref[...]).astype(BF16)


def hub_pack_kernel(keep_ref, came_ref, out_ref):
    out_ref[...] = (keep_ref[...] + came_ref[...]).astype(BF16)


def weights_kernel(core, feat_ref, agg_ref, cot_ref, keep_ref, send_ref, acc):
    step = pl.program_id(0)
    first = contract(feat_ref[...], cot_ref[...], 0, 0)
    second = contract(agg_ref[...], cot_ref[...], 0, 0)

    @pl.when(step == 0)
    def _():
        acc[:WIDTH] = first
        acc[WIDTH:] = second

    @pl.when(step != 0)
    def _():
        acc[:WIDTH] += first
        acc[WIDTH:] += second

    def put(ref, column):
        for k in range(2):
            ref[k * 2 * WIDTH : (k + 1) * 2 * WIDTH, :] = acc[:, column + k * TILE : column + (k + 1) * TILE]

    last = step == pl.num_programs(0) - 1

    @pl.when(last & (core[0] == 0))
    def _():
        put(keep_ref, 0)
        put(send_ref, 2 * TILE)

    @pl.when(last & (core[0] != 0))
    def _():
        put(keep_ref, 2 * TILE)
        put(send_ref, 0)


def spread_kernel(arrived_ref, packed_hbm, out_ref):
    del packed_hbm
    for c in range(2):
        total = jnp.zeros((16, TILE), F32)
        for y in range(4):
            for m in range(16):
                start = (2 * y + c) * 256 + 16 * m
                total += arrived_ref[start : start + 16, :].astype(F32)
        total = total.astype(BF16)
        for peer in range(64):
            out_ref[16 * peer : 16 * peer + 16, c * TILE : (c + 1) * TILE] = total


def landing_kernel(targets_ref, own_ref, arrived_ref, nodes_ref):
    chunk = 256
    slots = arrived_ref.shape[0]
    for s in range(slots // chunk):
        goal = targets_ref[s : s + 1, :]
        place = (lax.broadcasted_iota(jnp.int32, (NODES, chunk), 0) == goal).astype(BF16)
        part = contract(place, arrived_ref[s * chunk : (s + 1) * chunk, :], 1, 0)
        if s == 0:
            nodes_ref[...] = own_ref[...] + part
        else:
            nodes_ref[...] += part


def hub_sum_kernel(arrived_ref, hubs_ref):
    total = jnp.zeros((16, WIDTH), F32)
    for p in range(64):
        total += arrived_ref[16 * p : 16 * p + 16, :].astype(F32)
    hubs_ref[...] = total


def join_kernel(core, mine_ref, came_ref, out_ref):
    for ref, part in ((mine_ref, core[0]), (came_ref, 1 - core[0])):
        place = pl.ds(pl.multiple_of(part * 256, 256), 256)
        for y in range(4):
            for c in range(2):
                column = (2 * c + y // 2) * TILE
                block = ref[y * 256 : (y + 1) * 256, c * TILE : (c + 1) * TILE]
                out_ref[y % 2, place, column : column + TILE] = block.astype(F32)


def whole(*shape):
    return pl.BlockSpec(shape, lambda i, *_: (0,) * len(shape))


ANY = pl.BlockSpec(memory_space=pl.ANY)


def call(kernel, name, scalars, ins, outs, shapes, scratch, flops, moved, grid=(1,), **more):
    return pl.pallas_call(
        kernel,
        grid_spec=pltpu.PrefetchScalarGridSpec(
            num_scalar_prefetch=scalars, grid=grid, in_specs=ins, out_specs=outs, scratch_shapes=scratch
        ),
        out_shape=shapes,
        compiler_params=pltpu.CompilerParams(vmem_limit_bytes=VMEM),
        cost_estimate=pl.CostEstimate(flops=flops, bytes_accessed=moved, transcendentals=0),
        name=name,
        **more,
    )


def tile_scratch(acc):
    kept = [pltpu.VMEM((REG + 1, TILE, TILE), BF16)]
    if acc:
        kept.append(pltpu.VMEM((HUB_BLOCKS * TILE, WIDTH), F32))
    return kept + [
        pltpu.VMEM((8, PLAN), jnp.int32),
        pltpu.SMEM((8, PLAN), jnp.int32),
        pltpu.SemaphoreType.DMA,
        pltpu.SemaphoreType.DMA,
    ]


def shift(k, n):
    return [(i, (i + k) % n) for i in range(n)]


def local(features, aggregated, cotangent, w_self, w_neigh, degrees, tile_rows, tile_cols, tile_vals, recv_rows):
    core_arg = lax.axis_index("core").reshape(1).astype(jnp.int32)
    rows = tile_rows.reshape(3, REG)
    cols = tile_cols.reshape(3, REG)
    deg = degrees.reshape(NODES // TILE, TILE)
    targets = recv_rows.reshape(8, 256)
    spec_rc = whole(3, REG)
    spec_nodes = whole(NODES, WIDTH)
    spec_w = whole(WIDTH, WIDTH)
    slots = HUB_BLOCKS * TILE
    region_flops = 2 * REG * TILE * TILE * WIDTH
    region_bytes = REG * TILE * TILE * 2 + NODES * WIDTH * 2 + slots * WIDTH * 2
    swap = shift(1, 2)

    steps = 4
    spec_rows = pl.BlockSpec((NODES // steps, WIDTH), lambda i, *_: (i, 0))
    w_keep, w_send = call(
        weights_kernel, "weights", 1, [spec_rows] * 3, [whole(slots, TILE)] * 2,
        [jax.ShapeDtypeStruct((slots, TILE), F32)] * 2, [pltpu.VMEM((2 * WIDTH, WIDTH), F32)],
        4 * NODES * WIDTH * WIDTH, 5 << 20, grid=(steps,),
    )(core_arg, features, aggregated, cotangent)
    w_came = lax.ppermute(w_send, "core", swap)

    wide = WIDTH + TILE
    msg, packed = call(
        ghost_kernel, "ghost", 0,
        [spec_rc, spec_rc, whole(8, TILE), spec_nodes, spec_w, ANY],
        [spec_nodes, whole(slots, WIDTH)],
        [jax.ShapeDtypeStruct((NODES, WIDTH), BF16), jax.ShapeDtypeStruct((slots, wide), BF16)],
        tile_scratch(True), region_flops + 2 * NODES * WIDTH * WIDTH, region_bytes + (2 << 20),
    )(rows, cols, deg, cotangent, w_neigh, tile_vals)
    spec_part = pl.BlockSpec((slots // steps, TILE), lambda i: (i, 0))
    packed = call(
        pack_kernel, "pack", 0, [spec_part, spec_part, ANY],
        pl.BlockSpec((slots // steps, TILE), lambda i: (i, WIDTH // TILE)),
        jax.ShapeDtypeStruct((slots, wide), BF16),
        [], slots * TILE, 3 << 20, grid=(steps,), input_output_aliases={2: 0},
    )(w_keep, w_came, packed)
    arrived = lax.all_to_all(
        packed.reshape(128, 16, wide), ALL, split_axis=0, concat_axis=0, tiled=True
    ).reshape(slots, wide)

    hub_keep, hub_send = call(
        hub_kernel, "hub", 1, [spec_rc, spec_rc, spec_nodes, ANY], [spec_nodes, spec_nodes],
        [jax.ShapeDtypeStruct((NODES, WIDTH), F32)] * 2,
        tile_scratch(True), region_flops, region_bytes + (2 << 20),
    )(core_arg, rows, cols, msg, tile_vals)
    hub_came = lax.ppermute(hub_send, "core", swap)
    own = call(
        own_kernel, "own", 0, [spec_rc, spec_rc, spec_nodes, spec_nodes, spec_w, ANY], spec_nodes,
        jax.ShapeDtypeStruct((NODES, WIDTH), F32),
        tile_scratch(False), region_flops + 2 * NODES * WIDTH * WIDTH, region_bytes,
    )(rows, cols, msg, cotangent, w_self, tile_vals)

    wider = WIDTH + 2 * TILE
    spec_hub = pl.BlockSpec((NODES // steps, WIDTH), lambda i: (i, 0))
    packed = call(
        hub_pack_kernel, "hub_pack", 0, [spec_hub, spec_hub], spec_hub,
        jax.ShapeDtypeStruct((NODES, wider), BF16), [], NODES * WIDTH, 5 << 20, grid=(steps,),
    )(hub_keep, hub_came)
    packed, own = lax.optimization_barrier((packed, own))
    packed = call(
        spread_kernel, "spread", 0, [pl.BlockSpec((slots, TILE), lambda i: (0, WIDTH // TILE)), ANY],
        pl.BlockSpec((NODES, 2 * TILE), lambda i: (0, WIDTH // (2 * TILE))),
        jax.ShapeDtypeStruct((NODES, wider), BF16), [], slots * TILE, 1 << 20, input_output_aliases={1: 0},
    )(arrived, packed)
    shared = lax.all_to_all(
        packed.reshape(64, 16, wider), ("y", "z", "x"), split_axis=0, concat_axis=0, tiled=True
    ).reshape(NODES, wider)

    grad_nodes = call(
        landing_kernel, "landing", 0, [whole(8, 256), spec_nodes, whole(slots, WIDTH)], spec_nodes,
        jax.ShapeDtypeStruct((NODES, WIDTH), F32), [], 2 * slots * NODES * WIDTH, 7 << 20,
    )(targets, own, arrived)

    shared, grad_nodes = lax.optimization_barrier((shared, grad_nodes))
    w_mine = shared[:, WIDTH:]
    w_theirs = lax.ppermute(w_mine, "core", swap)
    grad_hubs = call(
        hub_sum_kernel, "hub_sum", 0, [spec_nodes], whole(16, WIDTH),
        jax.ShapeDtypeStruct((16, WIDTH), F32), [], NODES * WIDTH, 1 << 20,
    )(shared)
    grad_weights = call(
        join_kernel, "join", 1, [whole(NODES, 2 * TILE)] * 2, whole(2, WIDTH, WIDTH),
        jax.ShapeDtypeStruct((2, WIDTH, WIDTH), F32), [], NODES * WIDTH, 3 << 20,
    )(core_arg, w_mine, w_theirs)
    return (grad_nodes, grad_hubs, grad_weights)


def solution(mesh):
    fine = Mesh(mesh.devices.reshape(4, 2, 4, 4), ALL)
    rows = P(ALL, None)
    in_specs = (
        rows, rows, rows, P(), P(), P(ALL), P(ALL), P(ALL), P(ALL, None, None), P(ALL, None, None),
    )
    out_specs = (rows, rows, P())
    return jax.shard_map(local, mesh=fine, in_specs=in_specs, out_specs=out_specs, check_vma=False)
```

```python
import functools

import jax
import jax.numpy as jnp
from jax import lax
from jax.experimental import pallas as pl
from jax.experimental.pallas import tpu as pltpu
from jax.sharding import Mesh, PartitionSpec as P

F32 = jnp.float32
BF16 = jnp.bfloat16
ALL = ("y", "core", "z", "x")
TILE = 128
REG = 128
WIDTH = 512
NODES = 1024
HUB_BLOCKS = 16
OWN_BLOCKS = 8
UNROLL = 8
PLAN = 256
LAYERS = 3
VMEM = 56 << 20


def contract(a, b, da, db):
    return lax.dot_general(a, b, (((da,), (db,)), ((), ())), preferred_element_type=F32)


def write_plan(region, rows_ref, cols_ref, plan_vmem, blocks):
    cols = cols_ref[region : region + 1, :]
    rows = rows_ref[region : region + 1, :]
    hot = (lax.broadcasted_iota(jnp.int32, (16, REG), 0) == cols).astype(F32)
    before = (
        lax.broadcasted_iota(jnp.int32, (REG, REG), 0) < lax.broadcasted_iota(jnp.int32, (REG, REG), 1)
    ).astype(BF16)
    rank = jnp.sum(hot * contract(hot.astype(BF16), before, 1, 0), axis=0, keepdims=True)
    counts = jnp.sum(hot, axis=1, keepdims=True)
    groups = jnp.floor((counts + 1.0) * 0.5)
    upto = (
        lax.broadcasted_iota(jnp.int32, (16, 16), 1) <= lax.broadcasted_iota(jnp.int32, (16, 16), 0)
    ).astype(BF16)
    ends = contract(upto, jnp.broadcast_to(groups, (16, REG)).astype(BF16), 1, 0)
    starts = ends - groups
    slot = 2.0 * jnp.sum(hot * starts, axis=0, keepdims=True) + rank
    match = (lax.broadcasted_iota(jnp.int32, (PLAN, REG), 0) == slot.astype(jnp.int32)).astype(BF16)
    which = lax.broadcasted_iota(jnp.int32, (8, REG), 1).astype(F32) - REG
    line = lax.broadcasted_iota(jnp.int32, (8, REG), 0)
    values = jnp.where(line == 0, which, jnp.where(line == 1, rows.astype(F32), 0.0))
    slots = contract(values.astype(BF16), match, 1, 1)
    group = lax.broadcasted_iota(jnp.int32, (16, REG), 1).astype(F32)
    column = jnp.sum((ends <= group).astype(F32), axis=0, keepdims=True)
    column = jnp.minimum(column, blocks - 1.0)
    column = jnp.concatenate([column, column], axis=1)
    line = lax.broadcasted_iota(jnp.int32, (8, PLAN), 0)
    plan_vmem[...] = jnp.where(line == 2, column, slots).astype(jnp.int32)


def tile_products(blocks, plan, vals, msg_ref, acc):
    groups = (REG + blocks) // 2

    def one(g):
        first = plan[0, 2 * g] + REG
        second = plan[0, 2 * g + 1] + REG
        row_a = pl.multiple_of(plan[1, 2 * g] * TILE, TILE)
        row_b = pl.multiple_of(plan[1, 2 * g + 1] * TILE, TILE)
        lhs = jnp.concatenate([vals[first], vals[second]], axis=0)
        rhs = jnp.concatenate([msg_ref[pl.ds(row_a, TILE), :], msg_ref[pl.ds(row_b, TILE), :]], axis=0)
        place = pl.ds(pl.multiple_of(plan[2, g] * TILE, TILE), TILE)
        acc[place, :] += contract(lhs, rhs, 0, 0)

    def body(step, carry):
        for k in range(UNROLL):
            one(step * UNROLL + k)
        return carry

    lax.fori_loop(0, groups // UNROLL, body, 0)
    for g in range(groups // UNROLL * UNROLL, groups):
        one(g)


def load_tiles(region, vals_hbm, vals, sem):
    copy = pltpu.make_async_copy(vals_hbm.at[pl.ds(region * REG, REG)], vals.at[pl.ds(0, REG)], sem)
    copy.start()
    vals[REG] = jnp.zeros((TILE, TILE), BF16)
    return copy


def make_plan(region, rows_ref, cols_ref, plan_vmem, plan, plan_sem, blocks):
    write_plan(region, rows_ref, cols_ref, plan_vmem, blocks)
    copy = pltpu.make_async_copy(plan_vmem, plan, plan_sem)
    copy.start()
    return copy


def write_cells(region, rows_ref, cols_ref, plan_vmem):
    cols = cols_ref[region : region + 1, :]
    rows = rows_ref[region : region + 1, :]
    cell = cols * (NODES // TILE) + rows
    hot = (lax.broadcasted_iota(jnp.int32, (REG, REG), 0) == cell).astype(F32)
    before = (
        lax.broadcasted_iota(jnp.int32, (REG, REG), 0) < lax.broadcasted_iota(jnp.int32, (REG, REG), 1)
    ).astype(BF16)
    rank = jnp.sum(hot * contract(hot.astype(BF16), before, 1, 0), axis=0, keepdims=True)
    line = lax.broadcasted_iota(jnp.int32, (8, REG), 0)
    which = lax.broadcasted_iota(jnp.int32, (8, REG), 1).astype(F32) - REG
    tables = jnp.zeros((8, REG), F32)
    for layer in range(LAYERS):
        value = jnp.where((line == layer) & (rank == layer), which, 0.0).astype(BF16)
        tables += contract(value, hot.astype(BF16), 1, 1)
    late = (rank >= LAYERS).astype(F32)
    place = contract(jnp.broadcast_to(late, (8, REG)).astype(BF16), before, 1, 0)[0:1, :]
    match = ((lax.broadcasted_iota(jnp.int32, (REG, REG), 0).astype(F32) == place) & (late > 0.0)).astype(BF16)
    value = jnp.where(line == 3, which, jnp.where(line == 4, rows.astype(F32), jnp.where(line == 5, cols.astype(F32), 0.0)))
    tables += contract(value.astype(BF16), match, 1, 1)
    tables = jnp.where(line == 6, jnp.sum(late, axis=1, keepdims=True), tables)
    plan_vmem[:, :REG] = tables.astype(jnp.int32)


def ghost_kernel(rows_ref, cols_ref, msg_hbm, keep_hbm, came_hbm, vals_hbm, out_hbm,
                 vals, msg, keep, came, dense, acc, out, plan_vmem, plan, sems, out_sems, plan_sem):
    copies = [
        pltpu.make_async_copy(
            vals_hbm.at[pl.ds(2 * REG + k * 32, 32)], vals.at[pl.ds(k * 32, 32)], sems.at[k]
        )
        for k in range(4)
    ]
    copies.append(pltpu.make_async_copy(msg_hbm, msg, sems.at[4]))
    copies.append(pltpu.make_async_copy(keep_hbm, keep, sems.at[5]))
    copies.append(pltpu.make_async_copy(came_hbm, came, sems.at[6]))
    for copy in copies:
        copy.start()
    vals[REG] = jnp.zeros((TILE, TILE), BF16)
    write_cells(2, rows_ref, cols_ref, plan_vmem)
    ready = pltpu.make_async_copy(plan_vmem, plan, plan_sem)
    ready.start()
    ready.wait()
    for copy in copies[:4]:
        copy.wait()
    per = NODES // TILE
    for c in range(HUB_BLOCKS):
        for r in range(per):
            total = vals[plan[0, c * per + r] + REG].astype(F32)
            for layer in range(1, LAYERS):
                total += vals[plan[layer, c * per + r] + REG].astype(F32)
            dense[c, r * TILE : (r + 1) * TILE, :] = total.astype(BF16)
    copies[4].wait()
    copies[5].wait()
    copies[6].wait()
    for b in range(4):
        lanes = slice(b * TILE, (b + 1) * TILE)
        out[b * WIDTH : (b + 1) * WIDTH, WIDTH:] = (keep[:, lanes] + came[:, lanes]).astype(BF16)
    for c in range(0, HUB_BLOCKS, 4):
        lhs = jnp.concatenate([dense[c + k] for k in range(4)], axis=1)
        acc[c * TILE : (c + 4) * TILE, :] = contract(lhs, msg[...], 0, 0)

    def late(k, carry):
        row = pl.multiple_of(plan[4, k] * TILE, TILE)
        place = pl.ds(pl.multiple_of(plan[5, k] * TILE, TILE), TILE)
        acc[place, :] += contract(vals[plan[3, k] + REG], msg[pl.ds(row, TILE), :], 0, 0)
        return carry

    lax.fori_loop(0, plan[6, 0], late, 0)
    sent = []
    piece = 4 * TILE
    for k in range(4):
        part = pl.ds(k * piece, piece)
        out[part, :WIDTH] = acc[part, :].astype(BF16)
        sent.append(pltpu.make_async_copy(out.at[part], out_hbm.at[part], out_sems.at[k]))
        sent[-1].start()
    for copy in sent:
        copy.wait()


def hub_kernel(core, rows_ref, cols_ref, msg_ref, vals_hbm, keep_ref, send_ref,
               vals, acc, plan_vmem, plan, sem, plan_sem):
    tiles = load_tiles(0, vals_hbm, vals, sem)
    ready = make_plan(0, rows_ref, cols_ref, plan_vmem, plan, plan_sem, HUB_BLOCKS)
    acc[...] = jnp.zeros_like(acc)
    ready.wait()
    tiles.wait()
    tile_products(HUB_BLOCKS, plan, vals, msg_ref, acc)
    for y in range(4):
        mine = pl.multiple_of((2 * y + core[0]) * 256, 256)
        theirs = pl.multiple_of((2 * y + 1 - core[0]) * 256, 256)
        keep_ref[y * 256 : (y + 1) * 256, :] = acc[pl.ds(mine, 256), :]
        send_ref[y * 256 : (y + 1) * 256, :] = acc[pl.ds(theirs, 256), :]


def own_kernel(rows_ref, cols_ref, msg_ref, cot_ref, w_ref, vals_hbm, out_ref, vals, plan_vmem, plan, sem, plan_sem):
    tiles = load_tiles(1, vals_hbm, vals, sem)
    ready = make_plan(1, rows_ref, cols_ref, plan_vmem, plan, plan_sem, OWN_BLOCKS)
    for r in range(NODES // TILE):
        block = slice(r * TILE, (r + 1) * TILE)
        out_ref[block, :] = contract(cot_ref[block, :], w_ref[...], 1, 1)
    ready.wait()
    tiles.wait()
    tile_products(OWN_BLOCKS, plan, vals, msg_ref, out_ref)


def hub_pack_kernel(keep_ref, came_ref, out_ref):
    out_ref[...] = (keep_ref[...] + came_ref[...]).astype(BF16)


def spread_kernel(arrived_ref, packed_hbm, out_ref):
    del packed_hbm
    for c in range(2):
        total = jnp.zeros((16, TILE), F32)
        for y in range(4):
            for m in range(16):
                start = (2 * y + c) * 256 + 16 * m
                total += arrived_ref[start : start + 16, :].astype(F32)
        total = total.astype(BF16)
        for peer in range(64):
            out_ref[16 * peer : 16 * peer + 16, c * TILE : (c + 1) * TILE] = total


def landing_kernel(targets_ref, own_ref, arrived_ref, nodes_ref):
    chunk = 256
    slots = arrived_ref.shape[0]
    for s in range(slots // chunk):
        goal = targets_ref[s : s + 1, :]
        place = (lax.broadcasted_iota(jnp.int32, (NODES, chunk), 0) == goal).astype(BF16)
        part = contract(place, arrived_ref[s * chunk : (s + 1) * chunk, :], 1, 0)
        if s == 0:
            nodes_ref[...] = own_ref[...] + part
        else:
            nodes_ref[...] += part


def hub_sum_kernel(arrived_ref, hubs_ref):
    total = jnp.zeros((16, WIDTH), F32)
    for p in range(64):
        total += arrived_ref[16 * p : 16 * p + 16, :].astype(F32)
    hubs_ref[...] = total


def join_kernel(core, mine_ref, came_ref, out_ref):
    for ref, part in ((mine_ref, core[0]), (came_ref, 1 - core[0])):
        place = pl.ds(pl.multiple_of(part * 256, 256), 256)
        for y in range(4):
            for c in range(2):
                block = ref[y * 256 : (y + 1) * 256, c * TILE : (c + 1) * TILE]
                out_ref[c, place, y * TILE : (y + 1) * TILE] = block.astype(F32)


def whole(*shape):
    return pl.BlockSpec(shape, lambda i, *_: (0,) * len(shape))


ANY = pl.BlockSpec(memory_space=pl.ANY)


def call(kernel, name, scalars, ins, outs, shapes, scratch, flops, moved, grid=(1,), **more):
    return pl.pallas_call(
        kernel,
        grid_spec=pltpu.PrefetchScalarGridSpec(
            num_scalar_prefetch=scalars, grid=grid, in_specs=ins, out_specs=outs, scratch_shapes=scratch
        ),
        out_shape=shapes,
        compiler_params=pltpu.CompilerParams(vmem_limit_bytes=VMEM),
        cost_estimate=pl.CostEstimate(flops=flops, bytes_accessed=moved, transcendentals=0),
        name=name,
        **more,
    )


def tile_scratch(acc):
    kept = [pltpu.VMEM((REG + 1, TILE, TILE), BF16)]
    if acc:
        kept.append(pltpu.VMEM((HUB_BLOCKS * TILE, WIDTH), F32))
    return kept + [
        pltpu.VMEM((8, PLAN), jnp.int32),
        pltpu.SMEM((8, PLAN), jnp.int32),
        pltpu.SemaphoreType.DMA,
        pltpu.SemaphoreType.DMA,
    ]


def shift(k, n):
    return [(i, (i + k) % n) for i in range(n)]


def local(features, aggregated, cotangent, w_self, w_neigh, degrees, tile_rows, tile_cols, tile_vals, recv_rows):
    core_arg = lax.axis_index("core").reshape(1).astype(jnp.int32)
    rows = tile_rows.reshape(3, REG)
    cols = tile_cols.reshape(3, REG)
    targets = recv_rows.reshape(8, 256)
    spec_rc = whole(3, REG)
    spec_nodes = whole(NODES, WIDTH)
    spec_w = whole(WIDTH, WIDTH)
    slots = HUB_BLOCKS * TILE
    region_flops = 2 * REG * TILE * TILE * WIDTH
    region_bytes = REG * TILE * TILE * 2 + NODES * WIDTH * 2 + slots * WIDTH * 2
    swap = shift(1, 2)

    steps = 4
    core = lax.axis_index("core")
    w_first = contract(features, cotangent, 0, 0)
    w_second = contract(aggregated, cotangent, 0, 0)
    w_keep = jnp.where(core == 0, w_first, w_second)
    w_came = lax.ppermute(jnp.where(core == 0, w_second, w_first), "core", swap)
    msg = (contract(cotangent, w_neigh, 1, 1) / degrees[:, None].astype(F32)).astype(BF16)

    wide = WIDTH + TILE
    packed = call(
        ghost_kernel, "ghost", 0,
        [spec_rc, spec_rc, ANY, ANY, ANY, ANY], ANY,
        jax.ShapeDtypeStruct((slots, wide), BF16),
        [
            pltpu.VMEM((REG + 1, TILE, TILE), BF16),
            pltpu.VMEM((NODES, WIDTH), BF16),
            pltpu.VMEM((WIDTH, WIDTH), F32),
            pltpu.VMEM((WIDTH, WIDTH), F32),
            pltpu.VMEM((HUB_BLOCKS, NODES, TILE), BF16),
            pltpu.VMEM((slots, WIDTH), F32),
            pltpu.VMEM((slots, wide), BF16),
            pltpu.VMEM((8, PLAN), jnp.int32),
            pltpu.SMEM((8, PLAN), jnp.int32),
            pltpu.SemaphoreType.DMA((7,)),
            pltpu.SemaphoreType.DMA((4,)),
            pltpu.SemaphoreType.DMA,
        ],
        region_flops, region_bytes + (2 << 20),
    )(rows, cols, msg, w_keep, w_came, tile_vals)
    arrived = lax.all_to_all(
        packed.reshape(128, 16, wide), ALL, split_axis=0, concat_axis=0, tiled=True
    ).reshape(slots, wide)

    hub_keep, hub_send = call(
        hub_kernel, "hub", 1, [spec_rc, spec_rc, spec_nodes, ANY], [spec_nodes, spec_nodes],
        [jax.ShapeDtypeStruct((NODES, WIDTH), F32)] * 2,
        tile_scratch(True), region_flops, region_bytes + (2 << 20),
    )(core_arg, rows, cols, msg, tile_vals)
    hub_came = lax.ppermute(hub_send, "core", swap)
    own = call(
        own_kernel, "own", 0, [spec_rc, spec_rc, spec_nodes, spec_nodes, spec_w, ANY], spec_nodes,
        jax.ShapeDtypeStruct((NODES, WIDTH), F32),
        tile_scratch(False), region_flops + 2 * NODES * WIDTH * WIDTH, region_bytes,
    )(rows, cols, msg, cotangent, w_self, tile_vals)

    wider = WIDTH + 2 * TILE
    spec_hub = pl.BlockSpec((NODES // steps, WIDTH), lambda i: (i, 0))
    packed = call(
        hub_pack_kernel, "hub_pack", 0, [spec_hub, spec_hub], spec_hub,
        jax.ShapeDtypeStruct((NODES, wider), BF16), [], NODES * WIDTH, 5 << 20, grid=(steps,),
    )(hub_keep, hub_came)
    packed, own = lax.optimization_barrier((packed, own))
    packed = call(
        spread_kernel, "spread", 0, [pl.BlockSpec((slots, TILE), lambda i: (0, WIDTH // TILE)), ANY],
        pl.BlockSpec((NODES, 2 * TILE), lambda i: (0, WIDTH // (2 * TILE))),
        jax.ShapeDtypeStruct((NODES, wider), BF16), [], slots * TILE, 1 << 20, input_output_aliases={1: 0},
    )(arrived, packed)
    shared = lax.all_to_all(
        packed.reshape(64, 16, wider), ("y", "z", "x"), split_axis=0, concat_axis=0, tiled=True
    ).reshape(NODES, wider)

    grad_nodes = call(
        landing_kernel, "landing", 0, [whole(8, 256), spec_nodes, whole(slots, WIDTH)], spec_nodes,
        jax.ShapeDtypeStruct((NODES, WIDTH), F32), [], 2 * slots * NODES * WIDTH, 7 << 20,
    )(targets, own, arrived)

    shared, grad_nodes = lax.optimization_barrier((shared, grad_nodes))
    w_mine = shared[:, WIDTH:]
    w_theirs = lax.ppermute(w_mine, "core", swap)
    grad_hubs = call(
        hub_sum_kernel, "hub_sum", 0, [spec_nodes], whole(16, WIDTH),
        jax.ShapeDtypeStruct((16, WIDTH), F32), [], NODES * WIDTH, 1 << 20,
    )(shared)
    grad_weights = call(
        join_kernel, "join", 1, [whole(NODES, 2 * TILE)] * 2, whole(2, WIDTH, WIDTH),
        jax.ShapeDtypeStruct((2, WIDTH, WIDTH), F32), [], NODES * WIDTH, 3 << 20,
    )(core_arg, w_mine, w_theirs)
    return (grad_nodes, grad_hubs, grad_weights)


def solution(mesh):
    fine = Mesh(mesh.devices.reshape(4, 2, 4, 4), ALL)
    rows = P(ALL, None)
    in_specs = (
        rows, rows, rows, P(), P(), P(ALL), P(ALL), P(ALL), P(ALL, None, None), P(ALL, None, None),
    )
    out_specs = (rows, rows, P())
    return jax.shard_map(local, mesh=fine, in_specs=in_specs, out_specs=out_specs, check_vma=False)
```

```python
import functools

import jax
import jax.numpy as jnp
from jax import lax
from jax.experimental import pallas as pl
from jax.experimental.pallas import tpu as pltpu
from jax.sharding import Mesh, PartitionSpec as P

F32 = jnp.float32
BF16 = jnp.bfloat16
ALL = ("y", "core", "z", "x")
TILE = 128
REG = 128
WIDTH = 512
NODES = 1024
HUB_BLOCKS = 16
OWN_BLOCKS = 8
UNROLL = 8
PLAN = 256
LAYERS = 3
VMEM = 28 << 20


def contract(a, b, da, db):
    return lax.dot_general(a, b, (((da,), (db,)), ((), ())), preferred_element_type=F32)


def write_plan(region, rows_ref, cols_ref, plan_vmem, blocks):
    cols = cols_ref[region : region + 1, :]
    rows = rows_ref[region : region + 1, :]
    hot = (lax.broadcasted_iota(jnp.int32, (16, REG), 0) == cols).astype(F32)
    before = (
        lax.broadcasted_iota(jnp.int32, (REG, REG), 0) < lax.broadcasted_iota(jnp.int32, (REG, REG), 1)
    ).astype(BF16)
    rank = jnp.sum(hot * contract(hot.astype(BF16), before, 1, 0), axis=0, keepdims=True)
    counts = jnp.sum(hot, axis=1, keepdims=True)
    groups = jnp.floor((counts + 1.0) * 0.5)
    upto = (
        lax.broadcasted_iota(jnp.int32, (16, 16), 1) <= lax.broadcasted_iota(jnp.int32, (16, 16), 0)
    ).astype(BF16)
    ends = contract(upto, jnp.broadcast_to(groups, (16, REG)).astype(BF16), 1, 0)
    starts = ends - groups
    slot = 2.0 * jnp.sum(hot * starts, axis=0, keepdims=True) + rank
    match = (lax.broadcasted_iota(jnp.int32, (PLAN, REG), 0) == slot.astype(jnp.int32)).astype(BF16)
    which = lax.broadcasted_iota(jnp.int32, (8, REG), 1).astype(F32) - REG
    line = lax.broadcasted_iota(jnp.int32, (8, REG), 0)
    values = jnp.where(line == 0, which, jnp.where(line == 1, rows.astype(F32), 0.0))
    slots = contract(values.astype(BF16), match, 1, 1)
    group = lax.broadcasted_iota(jnp.int32, (16, REG), 1).astype(F32)
    column = jnp.sum((ends <= group).astype(F32), axis=0, keepdims=True)
    column = jnp.minimum(column, blocks - 1.0)
    column = jnp.concatenate([column, column], axis=1)
    line = lax.broadcasted_iota(jnp.int32, (8, PLAN), 0)
    plan_vmem[...] = jnp.where(line == 2, column, slots).astype(jnp.int32)


def tile_products(blocks, plan, vals, msg_ref, acc):
    groups = (REG + blocks) // 2

    def one(g):
        first = plan[0, 2 * g] + REG
        second = plan[0, 2 * g + 1] + REG
        row_a = pl.multiple_of(plan[1, 2 * g] * TILE, TILE)
        row_b = pl.multiple_of(plan[1, 2 * g + 1] * TILE, TILE)
        lhs = jnp.concatenate([vals[first], vals[second]], axis=0)
        rhs = jnp.concatenate([msg_ref[pl.ds(row_a, TILE), :], msg_ref[pl.ds(row_b, TILE), :]], axis=0)
        place = pl.ds(pl.multiple_of(plan[2, g] * TILE, TILE), TILE)
        acc[place, :] += contract(lhs, rhs, 0, 0)

    def body(step, carry):
        for k in range(UNROLL):
            one(step * UNROLL + k)
        return carry

    lax.fori_loop(0, groups // UNROLL, body, 0)
    for g in range(groups // UNROLL * UNROLL, groups):
        one(g)


def load_tiles(region, vals_hbm, vals, sem):
    copy = pltpu.make_async_copy(vals_hbm.at[pl.ds(region * REG, REG)], vals.at[pl.ds(0, REG)], sem)
    copy.start()
    vals[REG] = jnp.zeros((TILE, TILE), BF16)
    return copy


def make_plan(region, rows_ref, cols_ref, plan_vmem, plan, plan_sem, blocks):
    write_plan(region, rows_ref, cols_ref, plan_vmem, blocks)
    copy = pltpu.make_async_copy(plan_vmem, plan, plan_sem)
    copy.start()
    return copy


def write_cells(region, rows_ref, cols_ref, plan_vmem):
    cols = cols_ref[region : region + 1, :]
    rows = rows_ref[region : region + 1, :]
    cell = cols * (NODES // TILE) + rows
    hot = (lax.broadcasted_iota(jnp.int32, (REG, REG), 0) == cell).astype(F32)
    before = (
        lax.broadcasted_iota(jnp.int32, (REG, REG), 0) < lax.broadcasted_iota(jnp.int32, (REG, REG), 1)
    ).astype(BF16)
    rank = jnp.sum(hot * contract(hot.astype(BF16), before, 1, 0), axis=0, keepdims=True)
    line = lax.broadcasted_iota(jnp.int32, (8, REG), 0)
    which = lax.broadcasted_iota(jnp.int32, (8, REG), 1).astype(F32) - REG
    tables = jnp.zeros((8, REG), F32)
    for layer in range(LAYERS):
        value = jnp.where((line == layer) & (rank == layer), which, 0.0).astype(BF16)
        tables += contract(value, hot.astype(BF16), 1, 1)
    late = (rank >= LAYERS).astype(F32)
    place = contract(jnp.broadcast_to(late, (8, REG)).astype(BF16), before, 1, 0)[0:1, :]
    match = ((lax.broadcasted_iota(jnp.int32, (REG, REG), 0).astype(F32) == place) & (late > 0.0)).astype(BF16)
    value = jnp.where(line == 3, which, jnp.where(line == 4, rows.astype(F32), jnp.where(line == 5, cols.astype(F32), 0.0)))
    tables += contract(value.astype(BF16), match, 1, 1)
    tables = jnp.where(line == 6, jnp.sum(late, axis=1, keepdims=True), tables)
    plan_vmem[:, :REG] = tables.astype(jnp.int32)


def ghost_kernel(rows_ref, cols_ref, msg, keep, came, vals_hbm, out_hbm,
                 vals, dense, acc, out, plan_vmem, plan, sem, out_sems, plan_sem):
    tiles = load_tiles(2, vals_hbm, vals, sem)
    write_cells(2, rows_ref, cols_ref, plan_vmem)
    ready = pltpu.make_async_copy(plan_vmem, plan, plan_sem)
    ready.start()
    for b in range(4):
        lanes = slice(b * TILE, (b + 1) * TILE)
        out[b * WIDTH : (b + 1) * WIDTH, WIDTH:] = (keep[:, lanes] + came[:, lanes]).astype(BF16)
    ready.wait()
    tiles.wait()
    per = NODES // TILE
    for c in range(HUB_BLOCKS):
        for r in range(per):
            total = vals[plan[0, c * per + r] + REG].astype(F32)
            for layer in range(1, LAYERS):
                total += vals[plan[layer, c * per + r] + REG].astype(F32)
            dense[c, r * TILE : (r + 1) * TILE, :] = total.astype(BF16)
    for c in range(0, HUB_BLOCKS, 4):
        lhs = jnp.concatenate([dense[c + k] for k in range(4)], axis=1)
        acc[c * TILE : (c + 4) * TILE, :] = contract(lhs, msg[...], 0, 0)

    def late(k, carry):
        row = pl.multiple_of(plan[4, k] * TILE, TILE)
        place = pl.ds(pl.multiple_of(plan[5, k] * TILE, TILE), TILE)
        acc[place, :] += contract(vals[plan[3, k] + REG], msg[pl.ds(row, TILE), :], 0, 0)
        return carry

    lax.fori_loop(0, plan[6, 0], late, 0)
    sent = []
    piece = 4 * TILE
    for k in range(4):
        part = pl.ds(k * piece, piece)
        out[part, :WIDTH] = acc[part, :].astype(BF16)
        sent.append(pltpu.make_async_copy(out.at[part], out_hbm.at[part], out_sems.at[k]))
        sent[-1].start()
    for copy in sent:
        copy.wait()


def hub_kernel(core, rows_ref, cols_ref, msg_ref, vals_hbm, keep_ref, send_ref,
               vals, acc, plan_vmem, plan, sem, plan_sem):
    tiles = load_tiles(0, vals_hbm, vals, sem)
    ready = make_plan(0, rows_ref, cols_ref, plan_vmem, plan, plan_sem, HUB_BLOCKS)
    acc[...] = jnp.zeros_like(acc)
    ready.wait()
    tiles.wait()
    tile_products(HUB_BLOCKS, plan, vals, msg_ref, acc)
    for y in range(4):
        mine = pl.multiple_of((2 * y + core[0]) * 256, 256)
        theirs = pl.multiple_of((2 * y + 1 - core[0]) * 256, 256)
        keep_ref[y * 256 : (y + 1) * 256, :] = acc[pl.ds(mine, 256), :]
        send_ref[y * 256 : (y + 1) * 256, :] = acc[pl.ds(theirs, 256), :]


def own_kernel(rows_ref, cols_ref, msg_ref, cot_ref, w_ref, vals_hbm, out_ref, vals, plan_vmem, plan, sem, plan_sem):
    tiles = load_tiles(1, vals_hbm, vals, sem)
    ready = make_plan(1, rows_ref, cols_ref, plan_vmem, plan, plan_sem, OWN_BLOCKS)
    for r in range(NODES // TILE):
        block = slice(r * TILE, (r + 1) * TILE)
        out_ref[block, :] = contract(cot_ref[block, :], w_ref[...], 1, 1)
    ready.wait()
    tiles.wait()
    tile_products(OWN_BLOCKS, plan, vals, msg_ref, out_ref)


def hub_pack_kernel(keep_ref, came_ref, out_ref):
    out_ref[...] = (keep_ref[...] + came_ref[...]).astype(BF16)


def spread_kernel(arrived_ref, packed_hbm, out_ref):
    del packed_hbm
    for c in range(2):
        total = jnp.zeros((16, TILE), F32)
        for y in range(4):
            for m in range(16):
                start = (2 * y + c) * 256 + 16 * m
                total += arrived_ref[start : start + 16, :].astype(F32)
        total = total.astype(BF16)
        for peer in range(64):
            out_ref[16 * peer : 16 * peer + 16, c * TILE : (c + 1) * TILE] = total


def landing_kernel(targets_ref, own_ref, arrived_ref, nodes_ref):
    chunk = 256
    slots = arrived_ref.shape[0]
    for s in range(slots // chunk):
        goal = targets_ref[s : s + 1, :]
        place = (lax.broadcasted_iota(jnp.int32, (NODES, chunk), 0) == goal).astype(BF16)
        part = contract(place, arrived_ref[s * chunk : (s + 1) * chunk, :], 1, 0)
        if s == 0:
            nodes_ref[...] = own_ref[...] + part
        else:
            nodes_ref[...] += part


def hub_sum_kernel(arrived_ref, hubs_ref):
    total = jnp.zeros((16, WIDTH), F32)
    for p in range(64):
        total += arrived_ref[16 * p : 16 * p + 16, :].astype(F32)
    hubs_ref[...] = total


def join_kernel(core, mine_ref, came_ref, out_ref):
    for ref, part in ((mine_ref, core[0]), (came_ref, 1 - core[0])):
        place = pl.ds(pl.multiple_of(part * 256, 256), 256)
        for y in range(4):
            for c in range(2):
                block = ref[y * 256 : (y + 1) * 256, c * TILE : (c + 1) * TILE]
                out_ref[c, place, y * TILE : (y + 1) * TILE] = block.astype(F32)


def whole(*shape):
    return pl.BlockSpec(shape, lambda i, *_: (0,) * len(shape))


ANY = pl.BlockSpec(memory_space=pl.ANY)
INSIDE = pl.BlockSpec(memory_space=pltpu.VMEM)
OUTSIDE = pl.BlockSpec(memory_space=pltpu.HBM)


def call(kernel, name, scalars, ins, outs, shapes, scratch, flops, moved, grid=(1,), **more):
    return pl.pallas_call(
        kernel,
        grid_spec=pltpu.PrefetchScalarGridSpec(
            num_scalar_prefetch=scalars, grid=grid, in_specs=ins, out_specs=outs, scratch_shapes=scratch
        ),
        out_shape=shapes,
        compiler_params=pltpu.CompilerParams(vmem_limit_bytes=VMEM),
        cost_estimate=pl.CostEstimate(flops=flops, bytes_accessed=moved, transcendentals=0),
        name=name,
        **more,
    )


def tile_scratch(acc):
    kept = [pltpu.VMEM((REG + 1, TILE, TILE), BF16)]
    if acc:
        kept.append(pltpu.VMEM((HUB_BLOCKS * TILE, WIDTH), F32))
    return kept + [
        pltpu.VMEM((8, PLAN), jnp.int32),
        pltpu.SMEM((8, PLAN), jnp.int32),
        pltpu.SemaphoreType.DMA,
        pltpu.SemaphoreType.DMA,
    ]


def shift(k, n):
    return [(i, (i + k) % n) for i in range(n)]


def local(features, aggregated, cotangent, w_self, w_neigh, degrees, tile_rows, tile_cols, tile_vals, recv_rows):
    core_arg = lax.axis_index("core").reshape(1).astype(jnp.int32)
    rows = tile_rows.reshape(3, REG)
    cols = tile_cols.reshape(3, REG)
    targets = recv_rows.reshape(8, 256)
    spec_rc = whole(3, REG)
    spec_nodes = whole(NODES, WIDTH)
    spec_w = whole(WIDTH, WIDTH)
    slots = HUB_BLOCKS * TILE
    region_flops = 2 * REG * TILE * TILE * WIDTH
    region_bytes = REG * TILE * TILE * 2 + NODES * WIDTH * 2 + slots * WIDTH * 2
    swap = shift(1, 2)
    tile_vals = pltpu.with_memory_space_constraint(tile_vals, pltpu.HBM)

    steps = 4
    core = lax.axis_index("core")
    w_first = contract(features, cotangent, 0, 0)
    w_second = contract(aggregated, cotangent, 0, 0)
    w_keep = jnp.where(core == 0, w_first, w_second)
    w_came = lax.ppermute(jnp.where(core == 0, w_second, w_first), "core", swap)
    msg = (contract(cotangent, w_neigh, 1, 1) / degrees[:, None].astype(F32)).astype(BF16)

    wide = WIDTH + TILE
    packed = call(
        ghost_kernel, "ghost", 0,
        [INSIDE] * 5 + [OUTSIDE], OUTSIDE,
        pltpu.HBM((slots, wide), BF16),
        [
            pltpu.VMEM((REG + 1, TILE, TILE), BF16),
            pltpu.VMEM((HUB_BLOCKS, NODES, TILE), BF16),
            pltpu.VMEM((slots, WIDTH), F32),
            pltpu.VMEM((slots, wide), BF16),
            pltpu.VMEM((8, PLAN), jnp.int32),
            pltpu.SMEM((8, PLAN), jnp.int32),
            pltpu.SemaphoreType.DMA,
            pltpu.SemaphoreType.DMA((4,)),
            pltpu.SemaphoreType.DMA,
        ],
        region_flops, region_bytes + (2 << 20), grid=(),
    )(rows, cols, msg, w_keep, w_came, tile_vals)
    arrived = lax.all_to_all(
        packed.reshape(128, 16, wide), ALL, split_axis=0, concat_axis=0, tiled=True
    ).reshape(slots, wide)

    hub_keep, hub_send = call(
        hub_kernel, "hub", 1, [spec_rc, spec_rc, spec_nodes, OUTSIDE], [spec_nodes, spec_nodes],
        [jax.ShapeDtypeStruct((NODES, WIDTH), F32)] * 2,
        tile_scratch(True), region_flops, region_bytes + (2 << 20),
    )(core_arg, rows, cols, msg, tile_vals)
    hub_came = lax.ppermute(hub_send, "core", swap)
    own = call(
        own_kernel, "own", 0, [spec_rc, spec_rc, spec_nodes, spec_nodes, spec_w, OUTSIDE], spec_nodes,
        jax.ShapeDtypeStruct((NODES, WIDTH), F32),
        tile_scratch(False), region_flops + 2 * NODES * WIDTH * WIDTH, region_bytes,
    )(rows, cols, msg, cotangent, w_self, tile_vals)

    wider = WIDTH + 2 * TILE
    spec_hub = pl.BlockSpec((NODES // steps, WIDTH), lambda i: (i, 0))
    packed = call(
        hub_pack_kernel, "hub_pack", 0, [spec_hub, spec_hub], spec_hub,
        jax.ShapeDtypeStruct((NODES, wider), BF16), [], NODES * WIDTH, 5 << 20, grid=(steps,),
    )(hub_keep, hub_came)
    packed, own = lax.optimization_barrier((packed, own))
    packed = call(
        spread_kernel, "spread", 0, [pl.BlockSpec((slots, TILE), lambda i: (0, WIDTH // TILE)), ANY],
        pl.BlockSpec((NODES, 2 * TILE), lambda i: (0, WIDTH // (2 * TILE))),
        jax.ShapeDtypeStruct((NODES, wider), BF16), [], slots * TILE, 1 << 20, input_output_aliases={1: 0},
    )(arrived, packed)
    shared = lax.all_to_all(
        packed.reshape(64, 16, wider), ("y", "z", "x"), split_axis=0, concat_axis=0, tiled=True
    ).reshape(NODES, wider)

    grad_nodes = call(
        landing_kernel, "landing", 0, [whole(8, 256), spec_nodes, whole(slots, WIDTH)], spec_nodes,
        jax.ShapeDtypeStruct((NODES, WIDTH), F32), [], 2 * slots * NODES * WIDTH, 7 << 20,
    )(targets, own, arrived)

    shared, grad_nodes = lax.optimization_barrier((shared, grad_nodes))
    w_mine = shared[:, WIDTH:]
    w_theirs = lax.ppermute(w_mine, "core", swap)
    grad_hubs = call(
        hub_sum_kernel, "hub_sum", 0, [spec_nodes], whole(16, WIDTH),
        jax.ShapeDtypeStruct((16, WIDTH), F32), [], NODES * WIDTH, 1 << 20,
    )(shared)
    grad_weights = call(
        join_kernel, "join", 1, [whole(NODES, 2 * TILE)] * 2, whole(2, WIDTH, WIDTH),
        jax.ShapeDtypeStruct((2, WIDTH, WIDTH), F32), [], NODES * WIDTH, 3 << 20,
    )(core_arg, w_mine, w_theirs)
    return (grad_nodes, grad_hubs, grad_weights)


def solution(mesh):
    fine = Mesh(mesh.devices.reshape(4, 2, 4, 4), ALL)
    rows = P(ALL, None)
    in_specs = (
        rows, rows, rows, P(), P(), P(ALL), P(ALL), P(ALL), P(ALL, None, None), P(ALL, None, None),
    )
    out_specs = (rows, rows, P())
    return jax.shard_map(local, mesh=fine, in_specs=in_specs, out_specs=out_specs, check_vma=False)
```

```python
import functools

import jax
import jax.numpy as jnp
from jax import lax
from jax.experimental import pallas as pl
from jax.experimental.pallas import tpu as pltpu
from jax.sharding import Mesh, PartitionSpec as P

F32 = jnp.float32
BF16 = jnp.bfloat16
ALL = ("y", "core", "z", "x")
TILE = 128
REG = 128
WIDTH = 512
NODES = 1024
HUB_BLOCKS = 16
OWN_BLOCKS = 8
UNROLL = 8
PLAN = 256
LAYERS = 4
VMEM = 28 << 20


def contract(a, b, da, db):
    return lax.dot_general(a, b, (((da,), (db,)), ((), ())), preferred_element_type=F32)


def write_plan(region, rows_ref, cols_ref, plan_vmem, blocks):
    cols = cols_ref[region : region + 1, :]
    rows = rows_ref[region : region + 1, :]
    hot = (lax.broadcasted_iota(jnp.int32, (16, REG), 0) == cols).astype(F32)
    before = (
        lax.broadcasted_iota(jnp.int32, (REG, REG), 0) < lax.broadcasted_iota(jnp.int32, (REG, REG), 1)
    ).astype(BF16)
    rank = jnp.sum(hot * contract(hot.astype(BF16), before, 1, 0), axis=0, keepdims=True)
    counts = jnp.sum(hot, axis=1, keepdims=True)
    groups = jnp.floor((counts + 1.0) * 0.5)
    upto = (
        lax.broadcasted_iota(jnp.int32, (16, 16), 1) <= lax.broadcasted_iota(jnp.int32, (16, 16), 0)
    ).astype(BF16)
    ends = contract(upto, jnp.broadcast_to(groups, (16, REG)).astype(BF16), 1, 0)
    starts = ends - groups
    slot = 2.0 * jnp.sum(hot * starts, axis=0, keepdims=True) + rank
    match = (lax.broadcasted_iota(jnp.int32, (PLAN, REG), 0) == slot.astype(jnp.int32)).astype(BF16)
    which = lax.broadcasted_iota(jnp.int32, (8, REG), 1).astype(F32) - REG
    line = lax.broadcasted_iota(jnp.int32, (8, REG), 0)
    values = jnp.where(line == 0, which, jnp.where(line == 1, rows.astype(F32), 0.0))
    slots = contract(values.astype(BF16), match, 1, 1)
    group = lax.broadcasted_iota(jnp.int32, (16, REG), 1).astype(F32)
    column = jnp.sum((ends <= group).astype(F32), axis=0, keepdims=True)
    column = jnp.minimum(column, blocks - 1.0)
    column = jnp.concatenate([column, column], axis=1)
    line = lax.broadcasted_iota(jnp.int32, (8, PLAN), 0)
    plan_vmem[...] = jnp.where(line == 2, column, slots).astype(jnp.int32)


def tile_products(blocks, plan, vals, msg_ref, acc):
    groups = (REG + blocks) // 2

    def one(g):
        first = plan[0, 2 * g] + REG
        second = plan[0, 2 * g + 1] + REG
        row_a = pl.multiple_of(plan[1, 2 * g] * TILE, TILE)
        row_b = pl.multiple_of(plan[1, 2 * g + 1] * TILE, TILE)
        lhs = jnp.concatenate([vals[first], vals[second]], axis=0)
        rhs = jnp.concatenate([msg_ref[pl.ds(row_a, TILE), :], msg_ref[pl.ds(row_b, TILE), :]], axis=0)
        place = pl.ds(pl.multiple_of(plan[2, g] * TILE, TILE), TILE)
        acc[place, :] += contract(lhs, rhs, 0, 0)

    def body(step, carry):
        for k in range(UNROLL):
            one(step * UNROLL + k)
        return carry

    lax.fori_loop(0, groups // UNROLL, body, 0)
    for g in range(groups // UNROLL * UNROLL, groups):
        one(g)


def load_tiles(region, vals_hbm, vals, sem):
    copy = pltpu.make_async_copy(vals_hbm.at[pl.ds(region * REG, REG)], vals.at[pl.ds(0, REG)], sem)
    copy.start()
    vals[REG] = jnp.zeros((TILE, TILE), BF16)
    return copy


def make_plan(region, rows_ref, cols_ref, plan_vmem, plan, plan_sem, blocks):
    write_plan(region, rows_ref, cols_ref, plan_vmem, blocks)
    copy = pltpu.make_async_copy(plan_vmem, plan, plan_sem)
    copy.start()
    return copy


def write_cells(region, rows_ref, cols_ref, plan_vmem):
    cols = cols_ref[region : region + 1, :]
    rows = rows_ref[region : region + 1, :]
    cell = cols * (NODES // TILE) + rows
    hot = (lax.broadcasted_iota(jnp.int32, (REG, REG), 0) == cell).astype(F32)
    before = (
        lax.broadcasted_iota(jnp.int32, (REG, REG), 0) < lax.broadcasted_iota(jnp.int32, (REG, REG), 1)
    ).astype(BF16)
    rank = jnp.sum(hot * contract(hot.astype(BF16), before, 1, 0), axis=0, keepdims=True)
    line = lax.broadcasted_iota(jnp.int32, (8, REG), 0)
    which = lax.broadcasted_iota(jnp.int32, (8, REG), 1).astype(F32) - REG
    tables = jnp.zeros((8, REG), F32)
    for layer in range(LAYERS):
        value = jnp.where((line == layer) & (rank == layer), which, 0.0).astype(BF16)
        tables += contract(value, hot.astype(BF16), 1, 1)
    late = (rank >= LAYERS).astype(F32)
    place = contract(jnp.broadcast_to(late, (8, REG)).astype(BF16), before, 1, 0)[0:1, :]
    match = ((lax.broadcasted_iota(jnp.int32, (REG, REG), 0).astype(F32) == place) & (late > 0.0)).astype(BF16)
    value = jnp.where(line == 4, which, jnp.where(line == 5, rows.astype(F32), jnp.where(line == 6, cols.astype(F32), 0.0)))
    tables += contract(value.astype(BF16), match, 1, 1)
    tables = jnp.where(line == 7, jnp.sum(late, axis=1, keepdims=True), tables)
    plan_vmem[:, :REG] = tables.astype(jnp.int32)


def ghost_kernel(rows_ref, cols_ref, msg, keep, came, vals_hbm, out_hbm,
                 vals, dense, acc, out, plan_vmem, plan, sem, out_sems, plan_sem):
    tiles = load_tiles(2, vals_hbm, vals, sem)
    write_cells(2, rows_ref, cols_ref, plan_vmem)
    ready = pltpu.make_async_copy(plan_vmem, plan, plan_sem)
    ready.start()
    for b in range(4):
        lanes = slice(b * TILE, (b + 1) * TILE)
        out[b * WIDTH : (b + 1) * WIDTH, WIDTH:] = (keep[:, lanes] + came[:, lanes]).astype(BF16)
    ready.wait()
    tiles.wait()
    per = NODES // TILE
    for c in range(HUB_BLOCKS):
        for r in range(per):
            total = vals[plan[0, c * per + r] + REG].astype(F32)
            for layer in range(1, LAYERS):
                total += vals[plan[layer, c * per + r] + REG].astype(F32)
            dense[c, r * TILE : (r + 1) * TILE, :] = total.astype(BF16)
    for c in range(0, HUB_BLOCKS, 4):
        lhs = jnp.concatenate([dense[c + k] for k in range(4)], axis=1)
        acc[c * TILE : (c + 4) * TILE, :] = contract(lhs, msg[...], 0, 0)

    def late(k, carry):
        row = pl.multiple_of(plan[5, k] * TILE, TILE)
        place = pl.ds(pl.multiple_of(plan[6, k] * TILE, TILE), TILE)
        acc[place, :] += contract(vals[plan[4, k] + REG], msg[pl.ds(row, TILE), :], 0, 0)
        return carry

    lax.fori_loop(0, plan[7, 0], late, 0)
    sent = []
    piece = 4 * TILE
    for k in range(4):
        part = pl.ds(k * piece, piece)
        out[part, :WIDTH] = acc[part, :].astype(BF16)
        sent.append(pltpu.make_async_copy(out.at[part], out_hbm.at[part], out_sems.at[k]))
        sent[-1].start()
    for copy in sent:
        copy.wait()


def hub_kernel(core, rows_ref, cols_ref, msg_ref, vals_hbm, keep_ref, send_ref,
               vals, acc, plan_vmem, plan, sem, plan_sem):
    tiles = load_tiles(0, vals_hbm, vals, sem)
    ready = make_plan(0, rows_ref, cols_ref, plan_vmem, plan, plan_sem, HUB_BLOCKS)
    acc[...] = jnp.zeros_like(acc)
    ready.wait()
    tiles.wait()
    tile_products(HUB_BLOCKS, plan, vals, msg_ref, acc)
    for y in range(4):
        mine = pl.multiple_of((2 * y + core[0]) * 256, 256)
        theirs = pl.multiple_of((2 * y + 1 - core[0]) * 256, 256)
        keep_ref[y * 256 : (y + 1) * 256, :] = acc[pl.ds(mine, 256), :]
        send_ref[y * 256 : (y + 1) * 256, :] = acc[pl.ds(theirs, 256), :]


def own_kernel(rows_ref, cols_ref, msg_ref, cot_ref, w_ref, vals_hbm, out_ref, vals, plan_vmem, plan, sem, plan_sem):
    tiles = load_tiles(1, vals_hbm, vals, sem)
    ready = make_plan(1, rows_ref, cols_ref, plan_vmem, plan, plan_sem, OWN_BLOCKS)
    for r in range(NODES // TILE):
        block = slice(r * TILE, (r + 1) * TILE)
        out_ref[block, :] = contract(cot_ref[block, :], w_ref[...], 1, 1)
    ready.wait()
    tiles.wait()
    tile_products(OWN_BLOCKS, plan, vals, msg_ref, out_ref)


def hub_pack_kernel(keep_ref, came_ref, out_ref):
    out_ref[...] = (keep_ref[...] + came_ref[...]).astype(BF16)


def spread_kernel(arrived_ref, packed_hbm, out_ref):
    del packed_hbm
    for c in range(2):
        total = jnp.zeros((16, TILE), F32)
        for y in range(4):
            for m in range(16):
                start = (2 * y + c) * 256 + 16 * m
                total += arrived_ref[start : start + 16, :].astype(F32)
        total = total.astype(BF16)
        for peer in range(64):
            out_ref[16 * peer : 16 * peer + 16, c * TILE : (c + 1) * TILE] = total


def landing_kernel(targets_ref, own_ref, arrived_ref, nodes_ref):
    chunk = 256
    slots = arrived_ref.shape[0]
    for s in range(slots // chunk):
        goal = targets_ref[s : s + 1, :]
        place = (lax.broadcasted_iota(jnp.int32, (NODES, chunk), 0) == goal).astype(BF16)
        part = contract(place, arrived_ref[s * chunk : (s + 1) * chunk, :], 1, 0)
        if s == 0:
            nodes_ref[...] = own_ref[...] + part
        else:
            nodes_ref[...] += part


def hub_sum_kernel(arrived_ref, hubs_ref):
    total = jnp.zeros((16, WIDTH), F32)
    for p in range(64):
        total += arrived_ref[16 * p : 16 * p + 16, :].astype(F32)
    hubs_ref[...] = total


def join_kernel(core, mine_ref, came_ref, out_ref):
    for ref, part in ((mine_ref, core[0]), (came_ref, 1 - core[0])):
        place = pl.ds(pl.multiple_of(part * 256, 256), 256)
        for y in range(4):
            for c in range(2):
                block = ref[y * 256 : (y + 1) * 256, c * TILE : (c + 1) * TILE]
                out_ref[c, place, y * TILE : (y + 1) * TILE] = block.astype(F32)


def whole(*shape):
    return pl.BlockSpec(shape, lambda i, *_: (0,) * len(shape))


ANY = pl.BlockSpec(memory_space=pl.ANY)
INSIDE = pl.BlockSpec(memory_space=pltpu.VMEM)
OUTSIDE = pl.BlockSpec(memory_space=pltpu.HBM)


def call(kernel, name, scalars, ins, outs, shapes, scratch, flops, moved, grid=(1,), **more):
    return pl.pallas_call(
        kernel,
        grid_spec=pltpu.PrefetchScalarGridSpec(
            num_scalar_prefetch=scalars, grid=grid, in_specs=ins, out_specs=outs, scratch_shapes=scratch
        ),
        out_shape=shapes,
        compiler_params=pltpu.CompilerParams(vmem_limit_bytes=VMEM),
        cost_estimate=pl.CostEstimate(flops=flops, bytes_accessed=moved, transcendentals=0),
        name=name,
        **more,
    )


def tile_scratch(acc):
    kept = [pltpu.VMEM((REG + 1, TILE, TILE), BF16)]
    if acc:
        kept.append(pltpu.VMEM((HUB_BLOCKS * TILE, WIDTH), F32))
    return kept + [
        pltpu.VMEM((8, PLAN), jnp.int32),
        pltpu.SMEM((8, PLAN), jnp.int32),
        pltpu.SemaphoreType.DMA,
        pltpu.SemaphoreType.DMA,
    ]


def shift(k, n):
    return [(i, (i + k) % n) for i in range(n)]


def local(features, aggregated, cotangent, w_self, w_neigh, degrees, tile_rows, tile_cols, tile_vals, recv_rows):
    core_arg = lax.axis_index("core").reshape(1).astype(jnp.int32)
    rows = tile_rows.reshape(3, REG)
    cols = tile_cols.reshape(3, REG)
    targets = recv_rows.reshape(8, 256)
    spec_rc = whole(3, REG)
    spec_nodes = whole(NODES, WIDTH)
    spec_w = whole(WIDTH, WIDTH)
    slots = HUB_BLOCKS * TILE
    region_flops = 2 * REG * TILE * TILE * WIDTH
    region_bytes = REG * TILE * TILE * 2 + NODES * WIDTH * 2 + slots * WIDTH * 2
    swap = shift(1, 2)
    tile_vals = pltpu.with_memory_space_constraint(tile_vals, pltpu.HBM)

    steps = 4
    core = lax.axis_index("core")
    w_send = contract(jnp.where(core == 0, aggregated, features), cotangent, 0, 0)
    w_came = lax.ppermute(w_send, "core", swap)
    w_keep = contract(jnp.where(core == 0, features, aggregated), cotangent, 0, 0)
    msg = (contract(cotangent, w_neigh, 1, 1) / degrees[:, None].astype(F32)).astype(BF16)

    wide = WIDTH + TILE
    packed = call(
        ghost_kernel, "ghost", 0,
        [INSIDE] * 5 + [OUTSIDE], OUTSIDE,
        pltpu.HBM((slots, wide), BF16),
        [
            pltpu.VMEM((REG + 1, TILE, TILE), BF16),
            pltpu.VMEM((HUB_BLOCKS, NODES, TILE), BF16),
            pltpu.VMEM((slots, WIDTH), F32),
            pltpu.VMEM((slots, wide), BF16),
            pltpu.VMEM((8, PLAN), jnp.int32),
            pltpu.SMEM((8, PLAN), jnp.int32),
            pltpu.SemaphoreType.DMA,
            pltpu.SemaphoreType.DMA((4,)),
            pltpu.SemaphoreType.DMA,
        ],
        region_flops, region_bytes + (2 << 20), grid=(),
    )(rows, cols, msg, w_keep, w_came, tile_vals)
    arrived = lax.all_to_all(
        packed.reshape(128, 16, wide), ALL, split_axis=0, concat_axis=0, tiled=True
    ).reshape(slots, wide)

    hub_keep, hub_send = call(
        hub_kernel, "hub", 1, [spec_rc, spec_rc, spec_nodes, OUTSIDE], [spec_nodes, spec_nodes],
        [jax.ShapeDtypeStruct((NODES, WIDTH), F32)] * 2,
        tile_scratch(True), region_flops, region_bytes + (2 << 20),
    )(core_arg, rows, cols, msg, tile_vals)
    hub_came = lax.ppermute(hub_send, "core", swap)
    own = call(
        own_kernel, "own", 0, [spec_rc, spec_rc, spec_nodes, spec_nodes, spec_w, OUTSIDE], spec_nodes,
        jax.ShapeDtypeStruct((NODES, WIDTH), F32),
        tile_scratch(False), region_flops + 2 * NODES * WIDTH * WIDTH, region_bytes,
    )(rows, cols, msg, cotangent, w_self, tile_vals)

    wider = WIDTH + 2 * TILE
    spec_hub = pl.BlockSpec((NODES // steps, WIDTH), lambda i: (i, 0))
    packed = call(
        hub_pack_kernel, "hub_pack", 0, [spec_hub, spec_hub], spec_hub,
        jax.ShapeDtypeStruct((NODES, wider), BF16), [], NODES * WIDTH, 5 << 20, grid=(steps,),
    )(hub_keep, hub_came)
    packed, own = lax.optimization_barrier((packed, own))
    packed = call(
        spread_kernel, "spread", 0, [pl.BlockSpec((slots, TILE), lambda i: (0, WIDTH // TILE)), ANY],
        pl.BlockSpec((NODES, 2 * TILE), lambda i: (0, WIDTH // (2 * TILE))),
        jax.ShapeDtypeStruct((NODES, wider), BF16), [], slots * TILE, 1 << 20, input_output_aliases={1: 0},
    )(arrived, packed)
    shared = lax.all_to_all(
        packed.reshape(64, 16, wider), ("y", "z", "x"), split_axis=0, concat_axis=0, tiled=True
    ).reshape(NODES, wider)

    grad_nodes = call(
        landing_kernel, "landing", 0, [whole(8, 256), spec_nodes, whole(slots, WIDTH)], spec_nodes,
        jax.ShapeDtypeStruct((NODES, WIDTH), F32), [], 2 * slots * NODES * WIDTH, 7 << 20,
    )(targets, own, arrived)

    shared, grad_nodes = lax.optimization_barrier((shared, grad_nodes))
    w_mine = shared[:, WIDTH:]
    w_theirs = lax.ppermute(w_mine, "core", swap)
    grad_hubs = call(
        hub_sum_kernel, "hub_sum", 0, [spec_nodes], whole(16, WIDTH),
        jax.ShapeDtypeStruct((16, WIDTH), F32), [], NODES * WIDTH, 1 << 20,
    )(shared)
    grad_weights = call(
        join_kernel, "join", 1, [whole(NODES, 2 * TILE)] * 2, whole(2, WIDTH, WIDTH),
        jax.ShapeDtypeStruct((2, WIDTH, WIDTH), F32), [], NODES * WIDTH, 3 << 20,
    )(core_arg, w_mine, w_theirs)
    return (grad_nodes, grad_hubs, grad_weights)


def solution(mesh):
    fine = Mesh(mesh.devices.reshape(4, 2, 4, 4), ALL)
    rows = P(ALL, None)
    in_specs = (
        rows, rows, rows, P(), P(), P(ALL), P(ALL), P(ALL), P(ALL, None, None), P(ALL, None, None),
    )
    out_specs = (rows, rows, P())
    return jax.shard_map(local, mesh=fine, in_specs=in_specs, out_specs=out_specs, check_vma=False)
```

```python
import functools

import jax
import jax.numpy as jnp
from jax import lax
from jax.experimental import pallas as pl
from jax.experimental.pallas import tpu as pltpu
from jax.sharding import Mesh, PartitionSpec as P

F32 = jnp.float32
BF16 = jnp.bfloat16
ALL = ("y", "core", "z", "x")
TILE = 128
REG = 128
WIDTH = 512
NODES = 1024
HUB_BLOCKS = 16
OWN_BLOCKS = 8
UNROLL = 8
PLAN = 256
LAYERS = 4


def contract(a, b, da, db):
    return lax.dot_general(a, b, (((da,), (db,)), ((), ())), preferred_element_type=F32)


def write_plan(region, rows_ref, cols_ref, plan_vmem, blocks):
    cols = cols_ref[region : region + 1, :]
    rows = rows_ref[region : region + 1, :]
    hot = (lax.broadcasted_iota(jnp.int32, (16, REG), 0) == cols).astype(F32)
    before = (
        lax.broadcasted_iota(jnp.int32, (REG, REG), 0) < lax.broadcasted_iota(jnp.int32, (REG, REG), 1)
    ).astype(BF16)
    rank = jnp.sum(hot * contract(hot.astype(BF16), before, 1, 0), axis=0, keepdims=True)
    counts = jnp.sum(hot, axis=1, keepdims=True)
    groups = jnp.floor((counts + 1.0) * 0.5)
    upto = (
        lax.broadcasted_iota(jnp.int32, (16, 16), 1) <= lax.broadcasted_iota(jnp.int32, (16, 16), 0)
    ).astype(BF16)
    ends = contract(upto, jnp.broadcast_to(groups, (16, REG)).astype(BF16), 1, 0)
    starts = ends - groups
    slot = 2.0 * jnp.sum(hot * starts, axis=0, keepdims=True) + rank
    match = (lax.broadcasted_iota(jnp.int32, (PLAN, REG), 0) == slot.astype(jnp.int32)).astype(BF16)
    which = lax.broadcasted_iota(jnp.int32, (8, REG), 1).astype(F32) - REG
    line = lax.broadcasted_iota(jnp.int32, (8, REG), 0)
    values = jnp.where(line == 0, which, jnp.where(line == 1, rows.astype(F32), 0.0))
    slots = contract(values.astype(BF16), match, 1, 1)
    group = lax.broadcasted_iota(jnp.int32, (16, REG), 1).astype(F32)
    column = jnp.sum((ends <= group).astype(F32), axis=0, keepdims=True)
    column = jnp.minimum(column, blocks - 1.0)
    column = jnp.concatenate([column, column], axis=1)
    line = lax.broadcasted_iota(jnp.int32, (8, PLAN), 0)
    plan_vmem[...] = jnp.where(line == 2, column, slots).astype(jnp.int32)


def tile_products(blocks, plan, vals, msg_ref, acc):
    groups = (REG + blocks) // 2

    def one(g):
        first = plan[0, 2 * g] + REG
        second = plan[0, 2 * g + 1] + REG
        row_a = pl.multiple_of(plan[1, 2 * g] * TILE, TILE)
        row_b = pl.multiple_of(plan[1, 2 * g + 1] * TILE, TILE)
        lhs = jnp.concatenate([vals[first], vals[second]], axis=0)
        rhs = jnp.concatenate([msg_ref[pl.ds(row_a, TILE), :], msg_ref[pl.ds(row_b, TILE), :]], axis=0)
        place = pl.ds(pl.multiple_of(plan[2, g] * TILE, TILE), TILE)
        acc[place, :] += contract(lhs, rhs, 0, 0)

    def body(step, carry):
        for k in range(UNROLL):
            one(step * UNROLL + k)
        return carry

    lax.fori_loop(0, groups // UNROLL, body, 0)
    for g in range(groups // UNROLL * UNROLL, groups):
        one(g)


def load_tiles(region, vals_hbm, vals, sem):
    copy = pltpu.make_async_copy(vals_hbm.at[pl.ds(region * REG, REG)], vals.at[pl.ds(0, REG)], sem)
    copy.start()
    vals[REG] = jnp.zeros((TILE, TILE), BF16)
    return copy


def make_plan(region, rows_ref, cols_ref, plan_vmem, plan, plan_sem, blocks):
    write_plan(region, rows_ref, cols_ref, plan_vmem, blocks)
    copy = pltpu.make_async_copy(plan_vmem, plan, plan_sem)
    copy.start()
    return copy


def write_cells(region, rows_ref, cols_ref, plan_vmem):
    cols = cols_ref[region : region + 1, :]
    rows = rows_ref[region : region + 1, :]
    across = (cols * (NODES // TILE) + rows).astype(F32)
    down = jnp.transpose(jnp.broadcast_to(across, (8, REG)))[:, 0:1]
    sub = lax.broadcasted_iota(jnp.int32, (REG, REG), 0).astype(F32)
    lane = lax.broadcasted_iota(jnp.int32, (REG, REG), 1).astype(F32)

    def total(mask):
        return jnp.sum(mask.astype(F32), axis=0, keepdims=True)

    rank = total((down == across) & (sub < lane))
    order = rank + total(down < across)
    count = total(down == lane)
    start = total(down < lane)
    hot = (sub == across).astype(F32)
    large = (count > LAYERS).astype(F32)
    spot = total((jnp.sum(hot, axis=1, keepdims=True) > LAYERS) & (sub < lane))
    line = lax.broadcasted_iota(jnp.int32, (8, REG), 0).astype(F32)
    index = lax.broadcasted_iota(jnp.int32, (8, REG), 1).astype(F32)
    layers = contract(jnp.where(line == rank, index - REG, 0.0).astype(BF16), hot.astype(BF16), 1, 1) + REG
    layers = jnp.where(large > 0.0, jnp.where(line == 0.0, REG + 1.0 + spot, 1.0 * REG), layers)
    order = contract(index.astype(BF16), (sub == order).astype(BF16), 1, 1)
    chosen = contract(index.astype(BF16), ((sub == spot).astype(F32) * large).astype(BF16), 1, 1)
    many = jnp.sum(large, axis=1, keepdims=True)
    other = jnp.where(line == 0.0, order, jnp.where(line == 1.0, chosen, jnp.where(line == 2.0, start, jnp.where(line == 3.0, count, many))))
    plan_vmem[:, :REG] = layers.astype(jnp.int32)
    plan_vmem[:, REG:] = other.astype(jnp.int32)


def ghost_kernel(rows_ref, cols_ref, msg, keep, came, vals_hbm, out_hbm,
                 vals, dense, out, plan_vmem, plan, sem, out_sems, plan_sem):
    tiles = load_tiles(2, vals_hbm, vals, sem)
    write_cells(2, rows_ref, cols_ref, plan_vmem)
    ready = pltpu.make_async_copy(plan_vmem, plan, plan_sem)
    ready.start()
    for b in range(4):
        lanes = slice(b * TILE, (b + 1) * TILE)
        out[b * WIDTH : (b + 1) * WIDTH, WIDTH:] = (keep[:, lanes] + came[:, lanes]).astype(BF16)
    ready.wait()
    tiles.wait()
    per = NODES // TILE

    def large(k, carry):
        cell = plan[1, REG + k]
        start = plan[2, REG + cell]

        def add(i, total):
            return total + vals[plan[0, REG + start + i]].astype(F32)

        total = lax.fori_loop(0, plan[3, REG + cell], add, jnp.zeros((TILE, TILE), F32))
        vals[REG + 1 + k] = total.astype(BF16)
        return carry

    lax.fori_loop(0, plan[4, REG], large, 0)
    sent = []
    for c in range(0, HUB_BLOCKS, 4):
        for k in range(4):
            for r in range(per):
                tile = (c + k) * per + r
                parts = [vals[plan[layer, tile]] for layer in range(LAYERS)]
                dense[c + k, r * TILE : (r + 1) * TILE, :] = ((parts[0].astype(F32) + parts[1].astype(F32)) + (parts[2].astype(F32) + parts[3].astype(F32))).astype(BF16)
        lhs = jnp.concatenate([dense[c + k] for k in range(4)], axis=1)
        part = pl.ds(c * TILE, 4 * TILE)
        out[part, :WIDTH] = contract(lhs, msg[...], 0, 0).astype(BF16)
        sent.append(pltpu.make_async_copy(out.at[part], out_hbm.at[part], out_sems.at[c // 4]))
        sent[-1].start()
    for copy in sent:
        copy.wait()


def hub_kernel(core, rows_ref, cols_ref, msg_ref, vals_hbm, keep_ref, send_ref,
               vals, acc, plan_vmem, plan, sem, plan_sem):
    tiles = load_tiles(0, vals_hbm, vals, sem)
    ready = make_plan(0, rows_ref, cols_ref, plan_vmem, plan, plan_sem, HUB_BLOCKS)
    acc[...] = jnp.zeros_like(acc)
    ready.wait()
    tiles.wait()
    tile_products(HUB_BLOCKS, plan, vals, msg_ref, acc)
    for y in range(4):
        mine = pl.multiple_of((2 * y + core[0]) * 256, 256)
        theirs = pl.multiple_of((2 * y + 1 - core[0]) * 256, 256)
        keep_ref[y * 256 : (y + 1) * 256, :] = acc[pl.ds(mine, 256), :]
        send_ref[y * 256 : (y + 1) * 256, :] = acc[pl.ds(theirs, 256), :]


def own_kernel(rows_ref, cols_ref, msg_ref, cot_ref, w_ref, vals_hbm, out_ref, vals, plan_vmem, plan, sem, plan_sem):
    tiles = load_tiles(1, vals_hbm, vals, sem)
    ready = make_plan(1, rows_ref, cols_ref, plan_vmem, plan, plan_sem, OWN_BLOCKS)
    for r in range(NODES // TILE):
        block = slice(r * TILE, (r + 1) * TILE)
        out_ref[block, :] = contract(cot_ref[block, :], w_ref[...], 1, 1)
    ready.wait()
    tiles.wait()
    tile_products(OWN_BLOCKS, plan, vals, msg_ref, out_ref)


def hub_pack_kernel(keep_ref, came_ref, out_ref):
    out_ref[...] = (keep_ref[...] + came_ref[...]).astype(BF16)


def spread_kernel(arrived_ref, packed_hbm, out_ref):
    del packed_hbm
    for c in range(2):
        total = jnp.zeros((16, TILE), F32)
        for y in range(4):
            for m in range(16):
                start = (2 * y + c) * 256 + 16 * m
                total += arrived_ref[start : start + 16, :].astype(F32)
        total = total.astype(BF16)
        for peer in range(64):
            out_ref[16 * peer : 16 * peer + 16, c * TILE : (c + 1) * TILE] = total


def landing_kernel(targets_ref, own_ref, arrived_ref, nodes_ref):
    chunk = 256
    slots = arrived_ref.shape[0]
    for s in range(slots // chunk):
        goal = targets_ref[s : s + 1, :]
        place = (lax.broadcasted_iota(jnp.int32, (NODES, chunk), 0) == goal).astype(BF16)
        part = contract(place, arrived_ref[s * chunk : (s + 1) * chunk, :], 1, 0)
        if s == 0:
            nodes_ref[...] = own_ref[...] + part
        else:
            nodes_ref[...] += part


def hub_sum_kernel(arrived_ref, hubs_ref):
    total = jnp.zeros((16, WIDTH), F32)
    for p in range(64):
        total += arrived_ref[16 * p : 16 * p + 16, :].astype(F32)
    hubs_ref[...] = total


def join_kernel(core, mine_ref, came_ref, out_ref):
    for ref, part in ((mine_ref, core[0]), (came_ref, 1 - core[0])):
        place = pl.ds(pl.multiple_of(part * 256, 256), 256)
        for y in range(4):
            for c in range(2):
                block = ref[y * 256 : (y + 1) * 256, c * TILE : (c + 1) * TILE]
                out_ref[c, place, y * TILE : (y + 1) * TILE] = block.astype(F32)


def whole(*shape):
    return pl.BlockSpec(shape, lambda i, *_: (0,) * len(shape))


ANY = pl.BlockSpec(memory_space=pl.ANY)
INSIDE = pl.BlockSpec(memory_space=pltpu.VMEM)
OUTSIDE = pl.BlockSpec(memory_space=pltpu.HBM)


def call(kernel, name, scalars, ins, outs, shapes, scratch, flops, moved, mib, grid=(1,), **more):
    return pl.pallas_call(
        kernel,
        grid_spec=pltpu.PrefetchScalarGridSpec(
            num_scalar_prefetch=scalars, grid=grid, in_specs=ins, out_specs=outs, scratch_shapes=scratch
        ),
        out_shape=shapes,
        compiler_params=pltpu.CompilerParams(vmem_limit_bytes=mib << 20),
        cost_estimate=pl.CostEstimate(flops=flops, bytes_accessed=moved, transcendentals=0),
        name=name,
        **more,
    )


def tile_scratch(acc):
    kept = [pltpu.VMEM((REG + 1, TILE, TILE), BF16)]
    if acc:
        kept.append(pltpu.VMEM((HUB_BLOCKS * TILE, WIDTH), F32))
    return kept + [
        pltpu.VMEM((8, PLAN), jnp.int32),
        pltpu.SMEM((8, PLAN), jnp.int32),
        pltpu.SemaphoreType.DMA,
        pltpu.SemaphoreType.DMA,
    ]


def shift(k, n):
    return [(i, (i + k) % n) for i in range(n)]


def local(features, aggregated, cotangent, w_self, w_neigh, degrees, tile_rows, tile_cols, tile_vals, recv_rows):
    core_arg = lax.axis_index("core").reshape(1).astype(jnp.int32)
    rows = tile_rows.reshape(3, REG)
    cols = tile_cols.reshape(3, REG)
    targets = recv_rows.reshape(8, 256)
    spec_rc = whole(3, REG)
    spec_nodes = whole(NODES, WIDTH)
    spec_w = whole(WIDTH, WIDTH)
    slots = HUB_BLOCKS * TILE
    region_flops = 2 * REG * TILE * TILE * WIDTH
    region_bytes = REG * TILE * TILE * 2 + NODES * WIDTH * 2 + slots * WIDTH * 2
    swap = shift(1, 2)
    tile_vals = pltpu.with_memory_space_constraint(tile_vals, pltpu.HBM)

    steps = 4
    core = lax.axis_index("core")
    w_send = contract(jnp.where(core == 0, aggregated, features), cotangent, 0, 0)
    w_came = lax.ppermute(w_send, "core", swap)
    w_keep = contract(jnp.where(core == 0, features, aggregated), cotangent, 0, 0)
    msg = (contract(cotangent, w_neigh, 1, 1) / degrees[:, None].astype(F32)).astype(BF16)

    wide = WIDTH + TILE
    packed = call(
        ghost_kernel, "ghost", 0,
        [INSIDE] * 5 + [OUTSIDE], OUTSIDE,
        pltpu.HBM((slots, wide), BF16),
        [
            pltpu.VMEM((REG + 32, TILE, TILE), BF16),
            pltpu.VMEM((HUB_BLOCKS, NODES, TILE), BF16),
            pltpu.VMEM((slots, wide), BF16),
            pltpu.VMEM((8, PLAN), jnp.int32),
            pltpu.SMEM((8, PLAN), jnp.int32),
            pltpu.SemaphoreType.DMA,
            pltpu.SemaphoreType.DMA((4,)),
            pltpu.SemaphoreType.DMA,
        ],
        region_flops, region_bytes + (2 << 20), 18, grid=(),
    )(rows, cols, msg, w_keep, w_came, tile_vals)
    arrived = lax.all_to_all(
        packed.reshape(128, 16, wide), ALL, split_axis=0, concat_axis=0, tiled=True
    ).reshape(slots, wide)
    arrived = pltpu.with_memory_space_constraint(arrived, pltpu.HBM)

    hub_keep, hub_send = call(
        hub_kernel, "hub", 1, [spec_rc, spec_rc, spec_nodes, OUTSIDE], [spec_nodes, spec_nodes],
        [jax.ShapeDtypeStruct((NODES, WIDTH), F32)] * 2,
        tile_scratch(True), region_flops, region_bytes + (2 << 20), 24,
    )(core_arg, rows, cols, msg, tile_vals)
    hub_came = lax.ppermute(hub_send, "core", swap)
    own = call(
        own_kernel, "own", 0, [spec_rc, spec_rc, spec_nodes, spec_nodes, spec_w, OUTSIDE], spec_nodes,
        jax.ShapeDtypeStruct((NODES, WIDTH), F32),
        tile_scratch(False), region_flops + 2 * NODES * WIDTH * WIDTH, region_bytes, 20,
    )(rows, cols, msg, cotangent, w_self, tile_vals)

    wider = WIDTH + 2 * TILE
    spec_hub = pl.BlockSpec((NODES // steps, WIDTH), lambda i: (i, 0))
    packed = call(
        hub_pack_kernel, "hub_pack", 0, [spec_hub, spec_hub], spec_hub,
        jax.ShapeDtypeStruct((NODES, wider), BF16), [], NODES * WIDTH, 5 << 20, 8, grid=(steps,),
    )(hub_keep, hub_came)
    packed, own = lax.optimization_barrier((packed, own))
    packed = call(
        spread_kernel, "spread", 0, [pl.BlockSpec((slots, TILE), lambda i: (0, WIDTH // TILE)), ANY],
        pl.BlockSpec((NODES, 2 * TILE), lambda i: (0, WIDTH // (2 * TILE))),
        jax.ShapeDtypeStruct((NODES, wider), BF16), [], slots * TILE, 1 << 20, 6, input_output_aliases={1: 0},
    )(arrived, packed)
    shared = lax.all_to_all(
        packed.reshape(64, 16, wider), ("y", "z", "x"), split_axis=0, concat_axis=0, tiled=True
    ).reshape(NODES, wider)

    grad_nodes = call(
        landing_kernel, "landing", 0, [whole(8, 256), spec_nodes, whole(slots, WIDTH)], spec_nodes,
        jax.ShapeDtypeStruct((NODES, WIDTH), F32), [], 2 * slots * NODES * WIDTH, 7 << 20, 18,
    )(targets, own, arrived)

    shared, grad_nodes = lax.optimization_barrier((shared, grad_nodes))
    w_mine = shared[:, WIDTH:]
    w_theirs = lax.ppermute(w_mine, "core", swap)
    grad_hubs = call(
        hub_sum_kernel, "hub_sum", 0, [spec_nodes], whole(16, WIDTH),
        jax.ShapeDtypeStruct((16, WIDTH), F32), [], NODES * WIDTH, 1 << 20, 6,
    )(shared)
    grad_weights = call(
        join_kernel, "join", 1, [whole(NODES, 2 * TILE)] * 2, whole(2, WIDTH, WIDTH),
        jax.ShapeDtypeStruct((2, WIDTH, WIDTH), F32), [], NODES * WIDTH, 3 << 20, 10,
    )(core_arg, w_mine, w_theirs)
    return (grad_nodes, grad_hubs, grad_weights)


def solution(mesh):
    fine = Mesh(mesh.devices.reshape(4, 2, 4, 4), ALL)
    rows = P(ALL, None)
    in_specs = (
        rows, rows, rows, P(), P(), P(ALL), P(ALL), P(ALL), P(ALL, None, None), P(ALL, None, None),
    )
    out_specs = (rows, rows, P())
    return jax.shard_map(local, mesh=fine, in_specs=in_specs, out_specs=out_specs, check_vma=False)
```

```python
import functools

import jax
import jax.numpy as jnp
from jax import lax
from jax.experimental import pallas as pl
from jax.experimental.pallas import tpu as pltpu
from jax.sharding import Mesh, PartitionSpec as P

F32 = jnp.float32
BF16 = jnp.bfloat16
ALL = ("y", "core", "z", "x")
TILE = 128
REG = 128
WIDTH = 512
NODES = 1024
HUB_BLOCKS = 16
OWN_BLOCKS = 8
UNROLL = 8
PLAN = 256
LAYERS = 4


def contract(a, b, da, db):
    return lax.dot_general(a, b, (((da,), (db,)), ((), ())), preferred_element_type=F32)


def write_plan(region, rows_ref, cols_ref, plan_vmem, blocks):
    cols = cols_ref[region : region + 1, :]
    rows = rows_ref[region : region + 1, :]
    hot = (lax.broadcasted_iota(jnp.int32, (16, REG), 0) == cols).astype(F32)
    before = (
        lax.broadcasted_iota(jnp.int32, (REG, REG), 0) < lax.broadcasted_iota(jnp.int32, (REG, REG), 1)
    ).astype(BF16)
    rank = jnp.sum(hot * contract(hot.astype(BF16), before, 1, 0), axis=0, keepdims=True)
    counts = jnp.sum(hot, axis=1, keepdims=True)
    groups = jnp.floor((counts + 1.0) * 0.5)
    upto = (
        lax.broadcasted_iota(jnp.int32, (16, 16), 1) <= lax.broadcasted_iota(jnp.int32, (16, 16), 0)
    ).astype(BF16)
    ends = contract(upto, jnp.broadcast_to(groups, (16, REG)).astype(BF16), 1, 0)
    starts = ends - groups
    slot = 2.0 * jnp.sum(hot * starts, axis=0, keepdims=True) + rank
    match = (lax.broadcasted_iota(jnp.int32, (PLAN, REG), 0) == slot.astype(jnp.int32)).astype(BF16)
    which = lax.broadcasted_iota(jnp.int32, (8, REG), 1).astype(F32) - REG
    line = lax.broadcasted_iota(jnp.int32, (8, REG), 0)
    values = jnp.where(line == 0, which, jnp.where(line == 1, rows.astype(F32), 0.0))
    slots = contract(values.astype(BF16), match, 1, 1)
    group = lax.broadcasted_iota(jnp.int32, (16, REG), 1).astype(F32)
    column = jnp.sum((ends <= group).astype(F32), axis=0, keepdims=True)
    column = jnp.minimum(column, blocks - 1.0)
    column = jnp.concatenate([column, column], axis=1)
    line = lax.broadcasted_iota(jnp.int32, (8, PLAN), 0)
    plan_vmem[...] = jnp.where(line == 2, column, slots).astype(jnp.int32)


def tile_products(blocks, plan, vals, msg_ref, acc):
    groups = (REG + blocks) // 2

    def one(g):
        first = plan[0, 2 * g] + REG
        second = plan[0, 2 * g + 1] + REG
        row_a = pl.multiple_of(plan[1, 2 * g] * TILE, TILE)
        row_b = pl.multiple_of(plan[1, 2 * g + 1] * TILE, TILE)
        lhs = jnp.concatenate([vals[first], vals[second]], axis=0)
        rhs = jnp.concatenate([msg_ref[pl.ds(row_a, TILE), :], msg_ref[pl.ds(row_b, TILE), :]], axis=0)
        place = pl.ds(pl.multiple_of(plan[2, g] * TILE, TILE), TILE)
        acc[place, :] += contract(lhs, rhs, 0, 0)

    def body(step, carry):
        for k in range(UNROLL):
            one(step * UNROLL + k)
        return carry

    lax.fori_loop(0, groups // UNROLL, body, 0)
    for g in range(groups // UNROLL * UNROLL, groups):
        one(g)


def load_tiles(region, vals_hbm, vals, sem):
    copy = pltpu.make_async_copy(vals_hbm.at[pl.ds(region * REG, REG)], vals.at[pl.ds(0, REG)], sem)
    copy.start()
    vals[REG] = jnp.zeros((TILE, TILE), BF16)
    return copy


def make_plan(region, rows_ref, cols_ref, plan_vmem, plan, plan_sem, blocks):
    write_plan(region, rows_ref, cols_ref, plan_vmem, blocks)
    copy = pltpu.make_async_copy(plan_vmem, plan, plan_sem)
    copy.start()
    return copy


def write_cells(region, rows_ref, cols_ref, plan_vmem):
    cols = cols_ref[region : region + 1, :]
    rows = rows_ref[region : region + 1, :]
    across = (cols * (NODES // TILE) + rows).astype(F32)
    down = jnp.transpose(jnp.broadcast_to(across, (8, REG)))[:, 0:1]
    sub = lax.broadcasted_iota(jnp.int32, (REG, REG), 0).astype(F32)
    lane = lax.broadcasted_iota(jnp.int32, (REG, REG), 1).astype(F32)

    def total(mask):
        return jnp.sum(mask.astype(F32), axis=0, keepdims=True)

    rank = total((down == across) & (sub < lane))
    order = rank + total(down < across)
    count = total(down == lane)
    start = total(down < lane)
    hot = (sub == across).astype(F32)
    large = (count > LAYERS).astype(F32)
    spot = total((jnp.sum(hot, axis=1, keepdims=True) > LAYERS) & (sub < lane))
    line = lax.broadcasted_iota(jnp.int32, (8, REG), 0).astype(F32)
    index = lax.broadcasted_iota(jnp.int32, (8, REG), 1).astype(F32)
    layers = contract(jnp.where(line == rank, index - REG, 0.0).astype(BF16), hot.astype(BF16), 1, 1) + REG
    layers = jnp.where(large > 0.0, jnp.where(line == 0.0, REG + 1.0 + spot, 1.0 * REG), layers)
    order = contract(index.astype(BF16), (sub == order).astype(BF16), 1, 1)
    chosen = contract(index.astype(BF16), ((sub == spot).astype(F32) * large).astype(BF16), 1, 1)
    many = jnp.sum(large, axis=1, keepdims=True)
    other = jnp.where(line == 0.0, order, jnp.where(line == 1.0, chosen, jnp.where(line == 2.0, start, jnp.where(line == 3.0, count, many))))
    plan_vmem[:, :REG] = layers.astype(jnp.int32)
    plan_vmem[:, REG:] = other.astype(jnp.int32)


def ghost_kernel(rows_ref, cols_ref, msg, keep, came, vals_hbm, out_hbm,
                 vals, dense, out, plan_vmem, plan, sem, out_sems, plan_sem):
    tiles = load_tiles(2, vals_hbm, vals, sem)
    write_cells(2, rows_ref, cols_ref, plan_vmem)
    ready = pltpu.make_async_copy(plan_vmem, plan, plan_sem)
    ready.start()
    for b in range(4):
        lanes = slice(b * TILE, (b + 1) * TILE)
        out[b * WIDTH : (b + 1) * WIDTH, WIDTH:] = (keep[:, lanes] + came[:, lanes]).astype(BF16)
    ready.wait()
    tiles.wait()
    per = NODES // TILE

    def large(k, carry):
        cell = plan[1, REG + k]
        start = plan[2, REG + cell]

        def add(i, total):
            return total + vals[plan[0, REG + start + i]].astype(F32)

        total = lax.fori_loop(0, plan[3, REG + cell], add, jnp.zeros((TILE, TILE), F32))
        vals[REG + 1 + k] = total.astype(BF16)
        return carry

    lax.fori_loop(0, plan[4, REG], large, 0)
    sent = []
    for c in range(0, HUB_BLOCKS, 4):
        for k in range(4):
            for r in range(per):
                tile = (c + k) * per + r
                parts = [vals[plan[layer, tile]] for layer in range(LAYERS)]
                dense[c + k, r * TILE : (r + 1) * TILE, :] = ((parts[0].astype(F32) + parts[1].astype(F32)) + (parts[2].astype(F32) + parts[3].astype(F32))).astype(BF16)
        lhs = jnp.concatenate([dense[c + k] for k in range(4)], axis=1)
        part = pl.ds(c * TILE, 4 * TILE)
        out[part, :WIDTH] = contract(lhs, msg[...], 0, 0).astype(BF16)
        sent.append(pltpu.make_async_copy(out.at[part], out_hbm.at[part], out_sems.at[c // 4]))
        sent[-1].start()
    for copy in sent:
        copy.wait()


def hub_kernel(core, rows_ref, cols_ref, msg_ref, vals_hbm, keep_ref, send_ref,
               vals, acc, plan_vmem, plan, sem, plan_sem):
    tiles = load_tiles(0, vals_hbm, vals, sem)
    ready = make_plan(0, rows_ref, cols_ref, plan_vmem, plan, plan_sem, HUB_BLOCKS)
    acc[...] = jnp.zeros_like(acc)
    ready.wait()
    tiles.wait()
    tile_products(HUB_BLOCKS, plan, vals, msg_ref, acc)
    for y in range(4):
        mine = pl.multiple_of((2 * y + core[0]) * 256, 256)
        theirs = pl.multiple_of((2 * y + 1 - core[0]) * 256, 256)
        keep_ref[y * 256 : (y + 1) * 256, :] = acc[pl.ds(mine, 256), :]
        send_ref[y * 256 : (y + 1) * 256, :] = acc[pl.ds(theirs, 256), :]


def own_kernel(rows_ref, cols_ref, msg_ref, cot_ref, w_ref, vals_hbm, out_ref, vals, plan_vmem, plan, sem, plan_sem):
    tiles = load_tiles(1, vals_hbm, vals, sem)
    ready = make_plan(1, rows_ref, cols_ref, plan_vmem, plan, plan_sem, OWN_BLOCKS)
    for r in range(NODES // TILE):
        block = slice(r * TILE, (r + 1) * TILE)
        out_ref[block, :] = contract(cot_ref[block, :], w_ref[...], 1, 1)
    ready.wait()
    tiles.wait()
    tile_products(OWN_BLOCKS, plan, vals, msg_ref, out_ref)


def hub_pack_kernel(keep_ref, came_ref, out_ref):
    out_ref[...] = (keep_ref[...] + came_ref[...]).astype(BF16)


def spread_kernel(arrived_ref, packed_hbm, out_ref):
    del packed_hbm
    for c in range(2):
        total = jnp.zeros((16, TILE), F32)
        for y in range(4):
            for m in range(16):
                start = (2 * y + c) * 256 + 16 * m
                total += arrived_ref[start : start + 16, :].astype(F32)
        total = total.astype(BF16)
        for peer in range(64):
            out_ref[16 * peer : 16 * peer + 16, c * TILE : (c + 1) * TILE] = total


def landing_kernel(targets_ref, own_ref, arrived_ref, nodes_ref):
    chunk = 256
    slots = arrived_ref.shape[0]
    for s in range(slots // chunk):
        goal = targets_ref[s : s + 1, :]
        place = (lax.broadcasted_iota(jnp.int32, (NODES, chunk), 0) == goal).astype(BF16)
        part = contract(place, arrived_ref[s * chunk : (s + 1) * chunk, :], 1, 0)
        if s == 0:
            nodes_ref[...] = own_ref[...] + part
        else:
            nodes_ref[...] += part


def write_half(core, source_ref, lanes, half, sent, weights_hbm, sem):
    for y in range(4):
        for c in range(2):
            block = source_ref[y * 256 : (y + 1) * 256, lanes + c * TILE : lanes + (c + 1) * TILE]
            half[c, :, y * TILE : (y + 1) * TILE] = block.astype(F32)
    place = pl.ds(pl.multiple_of(core * 256, 256), 256)
    for c in range(2):
        sent.append(pltpu.make_async_copy(half.at[c], weights_hbm.at[c, place], sem.at[c]))
        sent[-1].start()


def finish_kernel(core, shared_ref, hubs_ref, weights_hbm, half, sem):
    sent = []
    write_half(core[0], shared_ref, WIDTH, half, sent, weights_hbm, sem)
    total = jnp.zeros((16, WIDTH), F32)
    for p in range(64):
        total += shared_ref[16 * p : 16 * p + 16, :WIDTH].astype(F32)
    hubs_ref[...] = total
    for copy in sent:
        copy.wait()


def join_kernel(core, came_ref, partial_hbm, weights_hbm, half, sem):
    del partial_hbm
    sent = []
    write_half(1 - core[0], came_ref, 0, half, sent, weights_hbm, sem)
    for copy in sent:
        copy.wait()


def whole(*shape):
    return pl.BlockSpec(shape, lambda i, *_: (0,) * len(shape))


ANY = pl.BlockSpec(memory_space=pl.ANY)
INSIDE = pl.BlockSpec(memory_space=pltpu.VMEM)
SCALAR = pl.BlockSpec(memory_space=pltpu.SMEM)
OUTSIDE = pl.BlockSpec(memory_space=pltpu.HBM)


def call(kernel, name, scalars, ins, outs, shapes, scratch, flops, moved, mib, grid=(1,), **more):
    return pl.pallas_call(
        kernel,
        grid_spec=pltpu.PrefetchScalarGridSpec(
            num_scalar_prefetch=scalars, grid=grid, in_specs=ins, out_specs=outs, scratch_shapes=scratch
        ),
        out_shape=shapes,
        compiler_params=pltpu.CompilerParams(vmem_limit_bytes=mib << 20),
        cost_estimate=pl.CostEstimate(flops=flops, bytes_accessed=moved, transcendentals=0),
        name=name,
        **more,
    )


def tile_scratch(acc):
    kept = [pltpu.VMEM((REG + 1, TILE, TILE), BF16)]
    if acc:
        kept.append(pltpu.VMEM((HUB_BLOCKS * TILE, WIDTH), F32))
    return kept + [
        pltpu.VMEM((8, PLAN), jnp.int32),
        pltpu.SMEM((8, PLAN), jnp.int32),
        pltpu.SemaphoreType.DMA,
        pltpu.SemaphoreType.DMA,
    ]


def shift(k, n):
    return [(i, (i + k) % n) for i in range(n)]


def local(features, aggregated, cotangent, w_self, w_neigh, degrees, tile_rows, tile_cols, tile_vals, recv_rows):
    core_arg = lax.axis_index("core").reshape(1).astype(jnp.int32)
    rows = tile_rows.reshape(3, REG)
    cols = tile_cols.reshape(3, REG)
    targets = recv_rows.reshape(8, 256)
    spec_rc = whole(3, REG)
    spec_nodes = whole(NODES, WIDTH)
    spec_w = whole(WIDTH, WIDTH)
    slots = HUB_BLOCKS * TILE
    region_flops = 2 * REG * TILE * TILE * WIDTH
    region_bytes = REG * TILE * TILE * 2 + NODES * WIDTH * 2 + slots * WIDTH * 2
    swap = shift(1, 2)
    tile_vals = pltpu.with_memory_space_constraint(tile_vals, pltpu.HBM)

    steps = 4
    core = lax.axis_index("core")
    w_send = contract(jnp.where(core == 0, aggregated, features), cotangent, 0, 0)
    w_came = lax.ppermute(w_send, "core", swap)
    w_keep = contract(jnp.where(core == 0, features, aggregated), cotangent, 0, 0)
    msg = (contract(cotangent, w_neigh, 1, 1) / degrees[:, None].astype(F32)).astype(BF16)

    wide = WIDTH + TILE
    packed = call(
        ghost_kernel, "ghost", 0,
        [INSIDE] * 5 + [OUTSIDE], OUTSIDE,
        pltpu.HBM((slots, wide), BF16),
        [
            pltpu.VMEM((REG + 32, TILE, TILE), BF16),
            pltpu.VMEM((HUB_BLOCKS, NODES, TILE), BF16),
            pltpu.VMEM((slots, wide), BF16),
            pltpu.VMEM((8, PLAN), jnp.int32),
            pltpu.SMEM((8, PLAN), jnp.int32),
            pltpu.SemaphoreType.DMA,
            pltpu.SemaphoreType.DMA((4,)),
            pltpu.SemaphoreType.DMA,
        ],
        region_flops, region_bytes + (2 << 20), 18, grid=(),
    )(rows, cols, msg, w_keep, w_came, tile_vals)
    arrived = lax.all_to_all(
        packed.reshape(128, 16, wide), ALL, split_axis=0, concat_axis=0, tiled=True
    ).reshape(slots, wide)
    arrived = pltpu.with_memory_space_constraint(arrived, pltpu.HBM)

    hub_keep, hub_send = call(
        hub_kernel, "hub", 1, [spec_rc, spec_rc, spec_nodes, OUTSIDE], [spec_nodes, spec_nodes],
        [jax.ShapeDtypeStruct((NODES, WIDTH), F32)] * 2,
        tile_scratch(True), region_flops, region_bytes + (2 << 20), 24,
    )(core_arg, rows, cols, msg, tile_vals)
    hub_came = lax.ppermute(hub_send, "core", swap)
    own = call(
        own_kernel, "own", 0, [spec_rc, spec_rc, spec_nodes, spec_nodes, spec_w, OUTSIDE], spec_nodes,
        jax.ShapeDtypeStruct((NODES, WIDTH), F32),
        tile_scratch(False), region_flops + 2 * NODES * WIDTH * WIDTH, region_bytes, 20,
    )(rows, cols, msg, cotangent, w_self, tile_vals)

    wider = WIDTH + 2 * TILE
    spec_hub = pl.BlockSpec((NODES // steps, WIDTH), lambda i: (i, 0))
    packed = call(
        hub_pack_kernel, "hub_pack", 0, [spec_hub, spec_hub], spec_hub,
        jax.ShapeDtypeStruct((NODES, wider), BF16), [], NODES * WIDTH, 5 << 20, 8, grid=(steps,),
    )(hub_keep, hub_came)
    packed, own = lax.optimization_barrier((packed, own))
    packed = call(
        spread_kernel, "spread", 0, [pl.BlockSpec((slots, TILE), lambda i: (0, WIDTH // TILE)), ANY],
        pl.BlockSpec((NODES, 2 * TILE), lambda i: (0, WIDTH // (2 * TILE))),
        jax.ShapeDtypeStruct((NODES, wider), BF16), [], slots * TILE, 1 << 20, 6, input_output_aliases={1: 0},
    )(arrived, packed)
    shared = lax.all_to_all(
        packed.reshape(64, 16, wider), ("y", "z", "x"), split_axis=0, concat_axis=0, tiled=True
    ).reshape(NODES, wider)

    grad_nodes = call(
        landing_kernel, "landing", 0, [whole(8, 256), spec_nodes, whole(slots, WIDTH)], spec_nodes,
        jax.ShapeDtypeStruct((NODES, WIDTH), F32), [], 2 * slots * NODES * WIDTH, 7 << 20, 18,
    )(targets, own, arrived)

    shared, grad_nodes = lax.optimization_barrier((shared, grad_nodes))
    w_mine = shared[:, WIDTH:]
    w_theirs = lax.ppermute(w_mine, "core", swap)
    half = [pltpu.VMEM((2, WIDTH // 2, WIDTH), F32), pltpu.SemaphoreType.DMA((2,))]
    grad_hubs, grad_weights = call(
        finish_kernel, "finish", 0, [SCALAR, INSIDE], [INSIDE, OUTSIDE],
        [jax.ShapeDtypeStruct((16, WIDTH), F32), pltpu.HBM((2, WIDTH, WIDTH), F32)],
        half, NODES * WIDTH, 3 << 20, 8, grid=(),
    )(core_arg, shared)
    grad_weights = call(
        join_kernel, "join", 0, [SCALAR, INSIDE, OUTSIDE], OUTSIDE, pltpu.HBM((2, WIDTH, WIDTH), F32),
        half, NODES * WIDTH, 2 << 20, 8, grid=(), input_output_aliases={2: 0},
    )(core_arg, w_theirs, pltpu.with_memory_space_constraint(grad_weights, pltpu.HBM))
    return (grad_nodes, grad_hubs, grad_weights)


def solution(mesh):
    fine = Mesh(mesh.devices.reshape(4, 2, 4, 4), ALL)
    rows = P(ALL, None)
    in_specs = (
        rows, rows, rows, P(), P(), P(ALL), P(ALL), P(ALL), P(ALL, None, None), P(ALL, None, None),
    )
    out_specs = (rows, rows, P())
    return jax.shard_map(local, mesh=fine, in_specs=in_specs, out_specs=out_specs, check_vma=False)
```

```python
import functools

import jax
import jax.numpy as jnp
from jax import lax
from jax.experimental import pallas as pl
from jax.experimental.pallas import tpu as pltpu
from jax.sharding import Mesh, PartitionSpec as P

F32 = jnp.float32
BF16 = jnp.bfloat16
ALL = ("y", "core", "z", "x")
TILE = 128
REG = 128
WIDTH = 512
NODES = 1024
HUB_BLOCKS = 16
OWN_BLOCKS = 8
UNROLL = 8
PLAN = 256
LAYERS = 3


def contract(a, b, da, db):
    return lax.dot_general(a, b, (((da,), (db,)), ((), ())), preferred_element_type=F32)


def write_plan(region, rows_ref, cols_ref, plan_vmem, blocks):
    cols = cols_ref[region : region + 1, :]
    rows = rows_ref[region : region + 1, :]
    hot = (lax.broadcasted_iota(jnp.int32, (16, REG), 0) == cols).astype(F32)
    before = (
        lax.broadcasted_iota(jnp.int32, (REG, REG), 0) < lax.broadcasted_iota(jnp.int32, (REG, REG), 1)
    ).astype(BF16)
    rank = jnp.sum(hot * contract(hot.astype(BF16), before, 1, 0), axis=0, keepdims=True)
    counts = jnp.sum(hot, axis=1, keepdims=True)
    groups = jnp.floor((counts + 1.0) * 0.5)
    upto = (
        lax.broadcasted_iota(jnp.int32, (16, 16), 1) <= lax.broadcasted_iota(jnp.int32, (16, 16), 0)
    ).astype(BF16)
    ends = contract(upto, jnp.broadcast_to(groups, (16, REG)).astype(BF16), 1, 0)
    starts = ends - groups
    slot = 2.0 * jnp.sum(hot * starts, axis=0, keepdims=True) + rank
    match = (lax.broadcasted_iota(jnp.int32, (PLAN, REG), 0) == slot.astype(jnp.int32)).astype(BF16)
    which = lax.broadcasted_iota(jnp.int32, (8, REG), 1).astype(F32) - REG
    line = lax.broadcasted_iota(jnp.int32, (8, REG), 0)
    values = jnp.where(line == 0, which, jnp.where(line == 1, rows.astype(F32), 0.0))
    slots = contract(values.astype(BF16), match, 1, 1)
    group = lax.broadcasted_iota(jnp.int32, (16, REG), 1).astype(F32)
    column = jnp.sum((ends <= group).astype(F32), axis=0, keepdims=True)
    column = jnp.minimum(column, blocks - 1.0)
    column = jnp.concatenate([column, column], axis=1)
    line = lax.broadcasted_iota(jnp.int32, (8, PLAN), 0)
    plan_vmem[...] = jnp.where(line == 2, column, slots).astype(jnp.int32)


def tile_products(blocks, plan, vals, msg_ref, acc):
    groups = (REG + blocks) // 2

    def one(g):
        first = plan[0, 2 * g] + REG
        second = plan[0, 2 * g + 1] + REG
        row_a = pl.multiple_of(plan[1, 2 * g] * TILE, TILE)
        row_b = pl.multiple_of(plan[1, 2 * g + 1] * TILE, TILE)
        lhs = jnp.concatenate([vals[first], vals[second]], axis=0)
        rhs = jnp.concatenate([msg_ref[pl.ds(row_a, TILE), :], msg_ref[pl.ds(row_b, TILE), :]], axis=0)
        place = pl.ds(pl.multiple_of(plan[2, g] * TILE, TILE), TILE)
        acc[place, :] += contract(lhs, rhs, 0, 0)

    def body(step, carry):
        for k in range(UNROLL):
            one(step * UNROLL + k)
        return carry

    lax.fori_loop(0, groups // UNROLL, body, 0)
    for g in range(groups // UNROLL * UNROLL, groups):
        one(g)


def load_tiles(region, vals_hbm, vals, sem):
    copy = pltpu.make_async_copy(vals_hbm.at[pl.ds(region * REG, REG)], vals.at[pl.ds(0, REG)], sem)
    copy.start()
    vals[REG] = jnp.zeros((TILE, TILE), BF16)
    return copy


def make_plan(region, rows_ref, cols_ref, plan_vmem, plan, plan_sem, blocks):
    write_plan(region, rows_ref, cols_ref, plan_vmem, blocks)
    copy = pltpu.make_async_copy(plan_vmem, plan, plan_sem)
    copy.start()
    return copy


def write_cells(region, rows_ref, cols_ref, plan_vmem):
    cols = cols_ref[region : region + 1, :]
    rows = rows_ref[region : region + 1, :]
    across = (cols * (NODES // TILE) + rows).astype(F32)
    down = jnp.transpose(jnp.broadcast_to(across, (8, REG)))[:, 0:1]
    sub = lax.broadcasted_iota(jnp.int32, (REG, REG), 0).astype(F32)
    lane = lax.broadcasted_iota(jnp.int32, (REG, REG), 1).astype(F32)

    def total(mask):
        return jnp.sum(mask.astype(F32), axis=0, keepdims=True)

    rank = total((down == across) & (sub < lane))
    order = rank + total(down < across)
    count = total(down == lane)
    start = total(down < lane)
    hot = (sub == across).astype(F32)
    large = (count > LAYERS).astype(F32)
    spot = total((jnp.sum(hot, axis=1, keepdims=True) > LAYERS) & (sub < lane))
    line = lax.broadcasted_iota(jnp.int32, (8, REG), 0).astype(F32)
    index = lax.broadcasted_iota(jnp.int32, (8, REG), 1).astype(F32)
    layers = contract(jnp.where(line == rank, index - REG, 0.0).astype(BF16), hot.astype(BF16), 1, 1) + REG
    layers = jnp.where(large > 0.0, jnp.where(line == 0.0, REG + 1.0 + spot, 1.0 * REG), layers)
    order = contract(index.astype(BF16), (sub == order).astype(BF16), 1, 1)
    chosen = contract(index.astype(BF16), ((sub == spot).astype(F32) * large).astype(BF16), 1, 1)
    many = jnp.sum(large, axis=1, keepdims=True)
    other = jnp.where(line == 0.0, order, jnp.where(line == 1.0, chosen, jnp.where(line == 2.0, start, jnp.where(line == 3.0, count, many))))
    plan_vmem[:, :REG] = layers.astype(jnp.int32)
    plan_vmem[:, REG:] = other.astype(jnp.int32)


def ready_kernel(rows_ref, cols_ref, deg_ref, cot_ref, w_ref, vals_hbm, msg, vals, tables, plan, sem, plan_sem):
    tiles = load_tiles(2, vals_hbm, vals, sem)
    write_cells(2, rows_ref, cols_ref, tables)
    ready = pltpu.make_async_copy(tables, plan, plan_sem)
    ready.start()
    scale = jnp.transpose(1.0 / deg_ref[...].astype(F32))
    for r in range(NODES // TILE):
        block = slice(r * TILE, (r + 1) * TILE)
        msg[block, :] = (contract(cot_ref[block, :], w_ref[...], 1, 1) * scale[:, r : r + 1]).astype(BF16)
    ready.wait()
    tiles.wait()

    def large(k, carry):
        cell = plan[1, REG + k]
        start = plan[2, REG + cell]

        def add(i, total):
            return total + vals[plan[0, REG + start + i]].astype(F32)

        total = lax.fori_loop(0, plan[3, REG + cell], add, jnp.zeros((TILE, TILE), F32))
        vals[REG + 1 + k] = total.astype(BF16)
        return carry

    lax.fori_loop(0, plan[4, REG], large, 0)


def ghost_kernel(plan, msg, keep, came, vals, out_hbm, dense, out, out_sems):
    per = NODES // TILE
    for b in range(4):
        lanes = slice(b * TILE, (b + 1) * TILE)
        out[b * WIDTH : (b + 1) * WIDTH, WIDTH:] = (keep[:, lanes] + came[:, lanes]).astype(BF16)
    sent = []
    for c in range(0, HUB_BLOCKS, 4):
        for k in range(4):
            for r in range(per):
                tile = (c + k) * per + r
                parts = [vals[plan[layer, tile]] for layer in range(LAYERS)]
                dense[c + k, r * TILE : (r + 1) * TILE, :] = (
                    (parts[0].astype(F32) + parts[1].astype(F32)) + parts[2].astype(F32)
                ).astype(BF16)
        lhs = jnp.concatenate([dense[c + k] for k in range(4)], axis=1)
        part = pl.ds(c * TILE, 4 * TILE)
        out[part, :WIDTH] = contract(lhs, msg[...], 0, 0).astype(BF16)
        sent.append(pltpu.make_async_copy(out.at[part], out_hbm.at[part], out_sems.at[c // 4]))
        sent[-1].start()
    for copy in sent:
        copy.wait()


def hub_kernel(core, rows_ref, cols_ref, msg_ref, vals_hbm, keep_ref, send_ref,
               vals, acc, plan_vmem, plan, sem, plan_sem):
    tiles = load_tiles(0, vals_hbm, vals, sem)
    ready = make_plan(0, rows_ref, cols_ref, plan_vmem, plan, plan_sem, HUB_BLOCKS)
    acc[...] = jnp.zeros_like(acc)
    ready.wait()
    tiles.wait()
    tile_products(HUB_BLOCKS, plan, vals, msg_ref, acc)
    for y in range(4):
        mine = pl.multiple_of((2 * y + core[0]) * 256, 256)
        theirs = pl.multiple_of((2 * y + 1 - core[0]) * 256, 256)
        keep_ref[y * 256 : (y + 1) * 256, :] = acc[pl.ds(mine, 256), :]
        send_ref[y * 256 : (y + 1) * 256, :] = acc[pl.ds(theirs, 256), :]


def own_kernel(rows_ref, cols_ref, msg_ref, cot_ref, w_ref, vals_hbm, out_ref, vals, plan_vmem, plan, sem, plan_sem):
    tiles = load_tiles(1, vals_hbm, vals, sem)
    ready = make_plan(1, rows_ref, cols_ref, plan_vmem, plan, plan_sem, OWN_BLOCKS)
    for r in range(NODES // TILE):
        block = slice(r * TILE, (r + 1) * TILE)
        out_ref[block, :] = contract(cot_ref[block, :], w_ref[...], 1, 1)
    ready.wait()
    tiles.wait()
    tile_products(OWN_BLOCKS, plan, vals, msg_ref, out_ref)


def hub_pack_kernel(keep_ref, came_ref, out_ref):
    out_ref[...] = (keep_ref[...] + came_ref[...]).astype(BF16)


def spread_kernel(arrived_ref, packed_hbm, out_ref):
    del packed_hbm
    for c in range(2):
        total = jnp.zeros((16, TILE), F32)
        for y in range(4):
            for m in range(16):
                start = (2 * y + c) * 256 + 16 * m
                total += arrived_ref[start : start + 16, :].astype(F32)
        total = total.astype(BF16)
        for peer in range(64):
            out_ref[16 * peer : 16 * peer + 16, c * TILE : (c + 1) * TILE] = total


def landing_kernel(targets_ref, own_ref, arrived_ref, nodes_ref):
    chunk = 256
    slots = arrived_ref.shape[0]
    for s in range(slots // chunk):
        goal = targets_ref[s : s + 1, :]
        place = (lax.broadcasted_iota(jnp.int32, (NODES, chunk), 0) == goal).astype(BF16)
        part = contract(place, arrived_ref[s * chunk : (s + 1) * chunk, :], 1, 0)
        if s == 0:
            nodes_ref[...] = own_ref[...] + part
        else:
            nodes_ref[...] += part


def write_half(core, source_ref, lanes, half, sent, weights_hbm, sem):
    for y in range(4):
        for c in range(2):
            block = source_ref[y * 256 : (y + 1) * 256, lanes + c * TILE : lanes + (c + 1) * TILE]
            half[c, :, y * TILE : (y + 1) * TILE] = block.astype(F32)
    place = pl.ds(pl.multiple_of(core * 256, 256), 256)
    for c in range(2):
        sent.append(pltpu.make_async_copy(half.at[c], weights_hbm.at[c, place], sem.at[c]))
        sent[-1].start()


def finish_kernel(core, shared_ref, hubs_ref, weights_hbm, half, sem):
    sent = []
    write_half(core[0], shared_ref, WIDTH, half, sent, weights_hbm, sem)
    total = jnp.zeros((16, WIDTH), F32)
    for p in range(64):
        total += shared_ref[16 * p : 16 * p + 16, :WIDTH].astype(F32)
    hubs_ref[...] = total
    for copy in sent:
        copy.wait()


def join_kernel(core, came_ref, partial_hbm, weights_hbm, half, sem):
    del partial_hbm
    sent = []
    write_half(1 - core[0], came_ref, 0, half, sent, weights_hbm, sem)
    for copy in sent:
        copy.wait()


def whole(*shape):
    return pl.BlockSpec(shape, lambda i, *_: (0,) * len(shape))


ANY = pl.BlockSpec(memory_space=pl.ANY)
INSIDE = pl.BlockSpec(memory_space=pltpu.VMEM)
SCALAR = pl.BlockSpec(memory_space=pltpu.SMEM)
OUTSIDE = pl.BlockSpec(memory_space=pltpu.HBM)


def call(kernel, name, scalars, ins, outs, shapes, scratch, flops, moved, mib, grid=(1,), **more):
    return pl.pallas_call(
        kernel,
        grid_spec=pltpu.PrefetchScalarGridSpec(
            num_scalar_prefetch=scalars, grid=grid, in_specs=ins, out_specs=outs, scratch_shapes=scratch
        ),
        out_shape=shapes,
        compiler_params=pltpu.CompilerParams(vmem_limit_bytes=mib << 20),
        cost_estimate=pl.CostEstimate(flops=flops, bytes_accessed=moved, transcendentals=0),
        name=name,
        **more,
    )


def tile_scratch(acc):
    kept = [pltpu.VMEM((REG + 1, TILE, TILE), BF16)]
    if acc:
        kept.append(pltpu.VMEM((HUB_BLOCKS * TILE, WIDTH), F32))
    return kept + [
        pltpu.VMEM((8, PLAN), jnp.int32),
        pltpu.SMEM((8, PLAN), jnp.int32),
        pltpu.SemaphoreType.DMA,
        pltpu.SemaphoreType.DMA,
    ]


def shift(k, n):
    return [(i, (i + k) % n) for i in range(n)]


def local(features, aggregated, cotangent, w_self, w_neigh, degrees, tile_rows, tile_cols, tile_vals, recv_rows):
    core_arg = lax.axis_index("core").reshape(1).astype(jnp.int32)
    rows = tile_rows.reshape(3, REG)
    cols = tile_cols.reshape(3, REG)
    targets = recv_rows.reshape(8, 256)
    spec_rc = whole(3, REG)
    spec_nodes = whole(NODES, WIDTH)
    spec_w = whole(WIDTH, WIDTH)
    slots = HUB_BLOCKS * TILE
    region_flops = 2 * REG * TILE * TILE * WIDTH
    region_bytes = REG * TILE * TILE * 2 + NODES * WIDTH * 2 + slots * WIDTH * 2
    swap = shift(1, 2)
    tile_vals = pltpu.with_memory_space_constraint(tile_vals, pltpu.HBM)

    steps = 4
    core = lax.axis_index("core")
    w_send = contract(jnp.where(core == 0, aggregated, features), cotangent, 0, 0)
    w_came = lax.ppermute(w_send, "core", swap)
    w_keep = contract(jnp.where(core == 0, features, aggregated), cotangent, 0, 0)
    msg, vals, tables = call(
        ready_kernel, "ready", 0, [INSIDE] * 5 + [OUTSIDE], [INSIDE] * 3,
        [
            pltpu.VMEM((NODES, WIDTH), BF16),
            pltpu.VMEM((REG + 40, TILE, TILE), BF16),
            jax.ShapeDtypeStruct((8, PLAN), jnp.int32),
        ],
        [pltpu.SMEM((8, PLAN), jnp.int32), pltpu.SemaphoreType.DMA, pltpu.SemaphoreType.DMA],
        2 * NODES * WIDTH * WIDTH, 6 << 20, 16, grid=(),
    )(rows, cols, degrees.reshape(NODES // TILE, TILE), cotangent, w_neigh, tile_vals)

    wide = WIDTH + TILE
    packed = call(
        ghost_kernel, "ghost", 0, [SCALAR] + [INSIDE] * 4, OUTSIDE,
        pltpu.HBM((slots, wide), BF16),
        [
            pltpu.VMEM((HUB_BLOCKS, NODES, TILE), BF16),
            pltpu.VMEM((slots, wide), BF16),
            pltpu.SemaphoreType.DMA((4,)),
        ],
        region_flops, region_bytes + (2 << 20), 18, grid=(),
    )(tables, msg, w_keep, w_came, vals)
    arrived = lax.all_to_all(
        packed.reshape(128, 16, wide), ALL, split_axis=0, concat_axis=0, tiled=True
    ).reshape(slots, wide)
    arrived = pltpu.with_memory_space_constraint(arrived, pltpu.HBM)

    hub_keep, hub_send = call(
        hub_kernel, "hub", 1, [spec_rc, spec_rc, spec_nodes, OUTSIDE], [spec_nodes, spec_nodes],
        [jax.ShapeDtypeStruct((NODES, WIDTH), F32)] * 2,
        tile_scratch(True), region_flops, region_bytes + (2 << 20), 24,
    )(core_arg, rows, cols, msg, tile_vals)
    hub_came = lax.ppermute(hub_send, "core", swap)
    own = call(
        own_kernel, "own", 0, [spec_rc, spec_rc, spec_nodes, spec_nodes, spec_w, OUTSIDE], spec_nodes,
        jax.ShapeDtypeStruct((NODES, WIDTH), F32),
        tile_scratch(False), region_flops + 2 * NODES * WIDTH * WIDTH, region_bytes, 20,
    )(rows, cols, msg, cotangent, w_self, tile_vals)

    wider = WIDTH + 2 * TILE
    spec_hub = pl.BlockSpec((NODES // steps, WIDTH), lambda i: (i, 0))
    packed = call(
        hub_pack_kernel, "hub_pack", 0, [spec_hub, spec_hub], spec_hub,
        jax.ShapeDtypeStruct((NODES, wider), BF16), [], NODES * WIDTH, 5 << 20, 8, grid=(steps,),
    )(hub_keep, hub_came)
    packed, own = lax.optimization_barrier((packed, own))
    packed = call(
        spread_kernel, "spread", 0, [pl.BlockSpec((slots, TILE), lambda i: (0, WIDTH // TILE)), ANY],
        pl.BlockSpec((NODES, 2 * TILE), lambda i: (0, WIDTH // (2 * TILE))),
        jax.ShapeDtypeStruct((NODES, wider), BF16), [], slots * TILE, 1 << 20, 6, input_output_aliases={1: 0},
    )(arrived, packed)
    shared = lax.all_to_all(
        packed.reshape(64, 16, wider), ("y", "z", "x"), split_axis=0, concat_axis=0, tiled=True
    ).reshape(NODES, wider)

    grad_nodes = call(
        landing_kernel, "landing", 0, [whole(8, 256), spec_nodes, whole(slots, WIDTH)], spec_nodes,
        jax.ShapeDtypeStruct((NODES, WIDTH), F32), [], 2 * slots * NODES * WIDTH, 7 << 20, 18,
    )(targets, own, arrived)

    shared, grad_nodes = lax.optimization_barrier((shared, grad_nodes))
    w_mine = shared[:, WIDTH:]
    w_theirs = lax.ppermute(w_mine, "core", swap)
    half = [pltpu.VMEM((2, WIDTH // 2, WIDTH), F32), pltpu.SemaphoreType.DMA((2,))]
    grad_hubs, grad_weights = call(
        finish_kernel, "finish", 0, [SCALAR, INSIDE], [INSIDE, OUTSIDE],
        [jax.ShapeDtypeStruct((16, WIDTH), F32), pltpu.HBM((2, WIDTH, WIDTH), F32)],
        half, NODES * WIDTH, 3 << 20, 8, grid=(),
    )(core_arg, shared)
    grad_weights = call(
        join_kernel, "join", 0, [SCALAR, INSIDE, OUTSIDE], OUTSIDE, pltpu.HBM((2, WIDTH, WIDTH), F32),
        half, NODES * WIDTH, 2 << 20, 8, grid=(), input_output_aliases={2: 0},
    )(core_arg, w_theirs, pltpu.with_memory_space_constraint(grad_weights, pltpu.HBM))
    return (grad_nodes, grad_hubs, grad_weights)


def solution(mesh):
    fine = Mesh(mesh.devices.reshape(4, 2, 4, 4), ALL)
    rows = P(ALL, None)
    in_specs = (
        rows, rows, rows, P(), P(), P(ALL), P(ALL), P(ALL), P(ALL, None, None), P(ALL, None, None),
    )
    out_specs = (rows, rows, P())
    return jax.shard_map(local, mesh=fine, in_specs=in_specs, out_specs=out_specs, check_vma=False)
```
